512 devices in a mesh: lon: 32 (over y_hi, z), lat: 16 (over x, y_lo, core).
Axes of the slice: x: 4, y: 4 (y_hi: 2, y_lo: 2; y = y_hi * 2 + y_lo), z: 16, core: 2. Of those that a mesh axis runs over, the one named last changes fastest.
Arguments:
- inputs: bfloat16 [2, 96, 384, 192], P(None, 'lat', 'lon'), may hold values from -6 to 6
- cotangent: bfloat16 [2, 96, 384, 192], P(None, 'lat', 'lon'), may hold values from -6 to 6
- w_qkv: bfloat16 [2, 192, 576], replicated, may hold values from -0.4375 to 0.4375
- w_proj: bfloat16 [2, 192, 192], replicated, may hold values from -0.4375 to 0.4375
- w_up: bfloat16 [2, 192, 768], replicated, may hold values from -0.4375 to 0.4375
- w_down: bfloat16 [2, 768, 192], replicated, may hold values from -0.21875 to 0.21875
- earth_bias: float32 [2, 16, 1, 6, 3312], P(None, 'lat'), may hold values from -4 to 392
Outputs:
- result: bfloat16 [2, 96, 384, 192], P(None, 'lat', 'lon')
- grad_inputs: bfloat16 [2, 96, 384, 192], P(None, 'lat', 'lon')
- grad_qkv: float32 [2, 192, 576], P(None, 'lon')
- grad_proj: float32 [2, 192, 192], P(None, 'lon')
- grad_up: float32 [2, 192, 768], P(None, 'lon')
- grad_down: float32 [2, 768, 192], P(None, 'lon')
- grad_bias: float32 [2, 16, 1, 6, 3312], P(None, 'lat')
The draws below stay inside these ranges and needn't reach their ends.
All inputs are finite; a program needn't handle non-finite values.
Results may differ from the reference program's by a relative error of at most 0.04.
Values may be sent and summed in bfloat16 or wider, within the bound.
A program may use at most 64 MiB of HBM per device.

```python
import jax
import jax.numpy as jnp
from jax import lax

C = 192
HEADS = 6
HID = 768
WZ = 2
WLAT = 6
WLON = 12
LEV = 2
NLAT = 96
NLON = 384
NLATW = 16
LEVW = 1


def draw_earth_bias(key, part):
    key = jax.random.fold_in(key, 7)
    base_key = jax.random.fold_in(key, 0)
    zone_len = WZ * WLAT
    reach_len = 2 * WLON - 1
    lead_shape = (2, NLATW, LEVW, HEADS)
    base_vals = jax.random.normal(base_key, lead_shape + (zone_len, zone_len, reach_len), jnp.float32)
    base_vals = jnp.clip(base_vals, -4.0, 4.0)
    return base_vals.reshape(lead_shape + (zone_len * zone_len * reach_len,))


def block_levels(own_key, dims, shards, low, largest):
    gain, own = 1.0, jax.random.fold_in(own_key, 6)
    for axis_at, parts in shards:
        heights = jnp.exp(jax.random.uniform(jax.random.fold_in(own, axis_at), (parts,), jnp.float32, low / len(shards), largest / len(shards)))
        gain = gain * jnp.repeat(heights, dims[axis_at] // parts).reshape([-1 if axis == axis_at else 1 for axis in range(len(dims))])
    return gain


def normal_values(stream_key, dims, deviation, limit, cuts=(), held_as=jnp.bfloat16):
    entries = jax.random.normal(stream_key, dims, jnp.float32) * deviation
    if len(cuts) > 0:
        entries = block_levels(stream_key, dims, cuts, -0.22, 0.18) * entries
    return jnp.clip(entries, min=-limit, max=limit).astype(held_as)


def setup_inputs(seed: int = 0) -> dict:
    streams_of = jax.random.split(jax.random.key(seed), 8)
    return {
        "inputs": normal_values(streams_of[0], (LEV, NLAT, NLON, C), 1.0, 6.0, ((1, 16), (2, 32))),
        "cotangent": normal_values(streams_of[1], (LEV, NLAT, NLON, C), 1.0, 6.0, ((1, 16), (2, 32))),
        "w_qkv": normal_values(streams_of[2], (2, C, 3 * C), C ** -0.5, 0.4375),
        "w_proj": normal_values(streams_of[3], (2, C, C), C ** -0.5, 0.4375),
        "w_up": normal_values(streams_of[4], (2, C, HID), C ** -0.5, 0.4375),
        "w_down": normal_values(streams_of[5], (2, HID, C), HID ** -0.5, 0.21875),
        "earth_bias": draw_earth_bias(jax.random.fold_in(streams_of[7], 71), 0),
    }


NEG_FILL = -1e+30
LN_EPS = 1e-05
INV_SQRT2 = 0.7071067811865476
INV_SQRT_2PI = 0.3989422804014327

def product(spec_text, left_side, right_side):
    return jnp.einsum(spec_text, left_side.astype(jnp.float32), right_side.astype(jnp.float32))

def outer_sum(left_side, right_side):
    left_flat = left_side.reshape(-1, left_side.shape[-1]).astype(jnp.float32)
    right_flat = right_side.reshape(-1, right_side.shape[-1]).astype(jnp.float32)
    return lax.dot_general(left_flat, right_flat, (((0,), (0,)), ((), ())))

def to_windows(grid_field):
    levels, lat_rows, lon_cols, feat_width = grid_field.shape
    shaped = grid_field.reshape(levels // WZ, WZ, lat_rows // WLAT, WLAT, lon_cols // WLON, WLON, feat_width)
    shaped = shaped.transpose(0, 2, 4, 1, 3, 5, 6)
    return shaped.reshape(levels // WZ, lat_rows // WLAT, lon_cols // WLON, WZ * WLAT * WLON, feat_width)

def from_windows(windows):
    lev_win, lat_win, lon_win, tokens_win, feat_width = windows.shape
    shaped = windows.reshape(lev_win, lat_win, lon_win, WZ, WLAT, WLON, feat_width)
    shaped = shaped.transpose(0, 3, 1, 4, 2, 5, 6)
    return shaped.reshape(lev_win * WZ, lat_win * WLAT, lon_win * WLON, feat_width)

def offset_table():
    query_lon = jnp.arange(WLON)[:, None, None]
    key_lon = jnp.arange(WLON)[None, :, None]
    offsets = jnp.arange(2 * WLON - 1)[None, None, :]
    return (key_lon - query_lon + WLON - 1 == offsets).astype(jnp.float32)

def expand_bias(bias_table, onehot):
    lead_shape = bias_table.shape[:-1]
    zone_len = WZ * WLAT
    shaped = bias_table.reshape(lead_shape + (zone_len, zone_len, 2 * WLON - 1))
    full_bias = jnp.einsum('...abr,ijr->...aibj', shaped, onehot, precision=lax.Precision.HIGHEST)
    return full_bias.reshape(lead_shape + (zone_len * WLON, zone_len * WLON))

def fold_bias(grad_full, onehot):
    lead_shape = grad_full.shape[:-2]
    zone_len = WZ * WLAT
    shaped = grad_full.reshape(lead_shape + (zone_len, WLON, zone_len, WLON))
    folded = jnp.einsum('...aibj,ijr->...abr', shaped, onehot, precision=lax.Precision.HIGHEST)
    return folded.reshape(lead_shape + (zone_len * zone_len * (2 * WLON - 1),))

def region_labels(levels_win, last_lat):
    token_pos = jnp.arange(WZ * WLAT * WLON)
    level_in = token_pos // (WLAT * WLON)
    lat_in = token_pos // WLON % WLAT
    lev_last = (jnp.arange(levels_win) == levels_win - 1)[:, None, None]
    level_part = lev_last & (level_in == WZ - 1)[None, None, :]
    lat_part = last_lat[None, :, None] & (lat_in >= WLAT // 2)[None, None, :]
    return level_part.astype(jnp.int32) * 2 + lat_part.astype(jnp.int32)

def normalize(values_in):
    mean_val = lax.optimization_barrier(jnp.mean(values_in, axis=-1, keepdims=True))
    centred = values_in - mean_val
    variance = lax.optimization_barrier(jnp.mean(centred * centred, axis=-1, keepdims=True))
    inv_std = lax.rsqrt(variance + LN_EPS)
    return (centred * inv_std, inv_std)

def normalize_back(scaled, inv_std, grad_out):
    mean_grad = lax.optimization_barrier(jnp.mean(grad_out, axis=-1, keepdims=True))
    mean_proj = lax.optimization_barrier(jnp.mean(grad_out * scaled, axis=-1, keepdims=True))
    return inv_std * (grad_out - mean_grad - scaled * mean_proj)

def gelu_exact(pre_vals):
    return 0.5 * pre_vals * (1.0 + lax.erf(pre_vals * INV_SQRT2))

def gelu_slope(pre_vals):
    return 0.5 * (1.0 + lax.erf(pre_vals * INV_SQRT2)) + pre_vals * jnp.exp(-0.5 * pre_vals * pre_vals) * INV_SQRT_2PI

def block_forward(windows, weights, win_bias, labels):
    w_qkv, w_proj, w_up, w_down = weights
    lead_shape = windows.shape[:-1]
    feat_width = windows.shape[-1]
    head_dim = feat_width // HEADS
    score_scale = head_dim ** (-0.5)
    inputs_f = windows.astype(jnp.float32)
    scaled_one, inv_one = normalize(inputs_f)
    normed_one = scaled_one.astype(jnp.bfloat16)
    packed = product('...c,cd->...d', normed_one, w_qkv).astype(jnp.bfloat16)
    packed = packed.reshape(lead_shape + (3, HEADS, head_dim))
    query_heads = packed[..., 0, :, :]
    key_heads = packed[..., 1, :, :]
    value_heads = packed[..., 2, :, :]
    scores = product('laophd,laoqhd->laohpq', query_heads, key_heads) * score_scale + win_bias[:, :, None]
    same_region = labels[:, :, None, None, :, None] == labels[:, :, None, None, None, :]
    scores = jnp.where(same_region, scores, NEG_FILL)
    row_top = lax.optimization_barrier(jnp.max(scores, axis=-1, keepdims=True))
    exp_scores = jnp.exp(scores - row_top)
    attn_probs = exp_scores / lax.optimization_barrier(jnp.sum(exp_scores, axis=-1, keepdims=True))
    attn_probs_b = attn_probs.astype(jnp.bfloat16)
    attn_mixed = product('laohpq,laoqhd->laophd', attn_probs_b, value_heads).astype(jnp.bfloat16)
    attn_mixed = attn_mixed.reshape(lead_shape + (feat_width,))
    hidden_f = inputs_f + product('...c,cd->...d', attn_mixed, w_proj)
    hidden_b = lax.optimization_barrier(hidden_f.astype(jnp.bfloat16))
    scaled_two, inv_two = normalize(hidden_b.astype(jnp.float32))
    normed_two = scaled_two.astype(jnp.bfloat16)
    pre_act = product('...c,ck->...k', normed_two, w_up)
    active = gelu_exact(pre_act).astype(jnp.bfloat16)
    output = (hidden_b.astype(jnp.float32) + product('...k,kc->...c', active, w_down)).astype(jnp.bfloat16)
    saved_acts = (normed_one, scaled_one, inv_one, query_heads, key_heads, value_heads, attn_probs, attn_probs_b, attn_mixed, scaled_two, inv_two, normed_two, pre_act, active)
    return (output, saved_acts)

def block_backward(grad_out, saved_acts, weights):
    normed_one, scaled_one, inv_one, query_heads, key_heads, value_heads, attn_probs, attn_probs_b, attn_mixed, scaled_two, inv_two, normed_two, pre_act, active = saved_acts
    w_qkv, w_proj, w_up, w_down = weights
    lead_shape = grad_out.shape[:-1]
    feat_width = grad_out.shape[-1]
    head_dim = feat_width // HEADS
    score_scale = head_dim ** (-0.5)
    grad_down = outer_sum(active, grad_out)
    grad_act = product('...c,kc->...k', grad_out, w_down)
    grad_pre = (grad_act * gelu_slope(pre_act)).astype(jnp.bfloat16)
    grad_up = outer_sum(normed_two, grad_pre)
    grad_norm_two = product('...k,ck->...c', grad_pre, w_up)
    grad_hidden = grad_out.astype(jnp.float32) + normalize_back(scaled_two, inv_two, grad_norm_two)
    grad_hidden_b = grad_hidden.astype(jnp.bfloat16)
    grad_proj = outer_sum(attn_mixed, grad_hidden_b)
    grad_mixed = product('...d,cd->...c', grad_hidden_b, w_proj).astype(jnp.bfloat16)
    grad_mixed = grad_mixed.reshape(lead_shape + (HEADS, head_dim))
    grad_probs = product('laophd,laoqhd->laohpq', grad_mixed, value_heads)
    grad_values = product('laohpq,laophd->laoqhd', attn_probs_b, grad_mixed)
    grad_scores = attn_probs * (grad_probs - lax.optimization_barrier(jnp.sum(grad_probs * attn_probs, axis=-1, keepdims=True)))
    grad_bias = lax.optimization_barrier(jnp.sum(grad_scores, axis=2))
    grad_scores_b = grad_scores.astype(jnp.bfloat16)
    grad_query = product('laohpq,laoqhd->laophd', grad_scores_b, key_heads) * score_scale
    grad_keys = product('laohpq,laophd->laoqhd', grad_scores_b, query_heads) * score_scale
    grad_packed = jnp.stack([grad_query, grad_keys, grad_values], axis=-3)
    grad_packed = grad_packed.reshape(lead_shape + (3 * feat_width,)).astype(jnp.bfloat16)
    grad_qkv = outer_sum(normed_one, grad_packed)
    grad_norm_one = product('...d,cd->...c', grad_packed, w_qkv)
    grad_in = (grad_hidden + normalize_back(scaled_one, inv_one, grad_norm_one)).astype(jnp.bfloat16)
    return (grad_in, (grad_qkv, grad_proj, grad_up, grad_down), grad_bias)

def by_rows(windows, win_bias, labels):
    return (windows.transpose(1, 0, 2, 3, 4)[:, :, None], win_bias.transpose(1, 0, 2, 3, 4)[:, :, None], labels.transpose(1, 0, 2)[:, :, None])

def forward_rows(windows, weights, win_bias, labels):

    def one_row(pieces):
        rows_in, row_bias, row_labels = pieces
        output, saved_acts = block_forward(rows_in, weights, row_bias, row_labels)
        return output
    outs = lax.map(one_row, by_rows(windows, win_bias, labels))
    return outs[:, :, 0].transpose(1, 0, 2, 3, 4)

def backward_rows(windows, grad_windows, weights, win_bias, labels, onehot):
    rows_in, rows_bias, rows_labels = by_rows(windows, win_bias, labels)
    rows_grad = grad_windows.transpose(1, 0, 2, 3, 4)[:, :, None]

    def one_row(pieces):
        row_in, row_grad, row_bias, row_labels = pieces
        output, saved_acts = block_forward(row_in, weights, row_bias, row_labels)
        return block_backward(row_grad, saved_acts, weights)
    grad_in, grads, grad_bias = lax.map(one_row, (rows_in, rows_grad, rows_bias, rows_labels))
    grad_in = grad_in[:, :, 0].transpose(1, 0, 2, 3, 4)
    grads = tuple((lax.optimization_barrier(jnp.sum(single, axis=0)) for single in grads))
    grad_bias = fold_bias(grad_bias[:, :, 0], onehot)
    return (grad_in, grads, grad_bias)

def reference(inputs, cotangent, w_qkv, w_proj, w_up, w_down, earth_bias):
    onehot = offset_table()
    levels_win = inputs.shape[0] // WZ
    lat_win = inputs.shape[1] // WLAT
    total_tokens = inputs.shape[0] * inputs.shape[1] * inputs.shape[2]
    norm_scale = total_tokens ** (-0.5)
    plain_labels = jnp.zeros((levels_win, lat_win, WZ * WLAT * WLON), jnp.int32)
    shift_labels = region_labels(levels_win, jnp.arange(lat_win).astype(jnp.int32) == lat_win - 1)
    weights_one = (w_qkv[0], w_proj[0], w_up[0], w_down[0])
    weights_two = (w_qkv[1], w_proj[1], w_up[1], w_down[1])
    bias_one = expand_bias(earth_bias[0], onehot).transpose(1, 0, 2, 3, 4)
    bias_two = expand_bias(earth_bias[1], onehot).transpose(1, 0, 2, 3, 4)
    shift_fwd = (-1, -(WLAT // 2), -(WLON // 2))
    shift_back = (1, WLAT // 2, WLON // 2)
    first_in = to_windows(inputs)
    middle = from_windows(forward_rows(first_in, weights_one, bias_one, plain_labels))
    second_in = to_windows(jnp.roll(middle, shift_fwd, axis=(0, 1, 2)))
    second_out = forward_rows(second_in, weights_two, bias_two, shift_labels)
    result = jnp.roll(from_windows(second_out), shift_back, axis=(0, 1, 2))
    grad_rolled = to_windows(jnp.roll(cotangent, shift_fwd, axis=(0, 1, 2)))
    grad_second, grads_two, bias_grad_two = backward_rows(second_in, grad_rolled, weights_two, bias_two, shift_labels, onehot)
    grad_mid = to_windows(jnp.roll(from_windows(grad_second), shift_back, axis=(0, 1, 2)))
    grad_first, grads_one, bias_grad_one = backward_rows(first_in, grad_mid, weights_one, bias_one, plain_labels, onehot)
    grad_inputs = from_windows(grad_first)
    stacked = tuple((jnp.stack([one_grad * norm_scale, two_grad * norm_scale]) for one_grad, two_grad in zip(grads_one, grads_two)))
    grad_bias = jnp.stack([bias_grad_one, bias_grad_two])
    return (result, grad_inputs, stacked[0], stacked[1], stacked[2], stacked[3], grad_bias)
```

```python
import jax
import jax.numpy as jnp
from jax import lax
from jax.experimental import pallas as pl
from jax.experimental.pallas import tpu as pltpu
from jax.sharding import PartitionSpec as P

BF = jnp.bfloat16
F32 = jnp.float32
MESH = pl.DeviceIdType.MESH

HEADS = 6
C = 192
HID = 768
WLON = 12
ZONES = 12
REACH = 23
TAB = ZONES * REACH
NLAT = 16
NLON = 32
SHARD = 6
TOK = 192
NEG_FILL = -1e30
LN_EPS = 1e-05
SCALE = 32.0 ** -0.5
NORM = 73728.0 ** -0.5

QPOS = [c if c < 6 else c + 2 for c in range(WLON)]
PAD_POS = [6, 7, 14, 15]


def nn(a, b):
    return lax.dot_general(a, b, (((1,), (0,)), ((), ())), preferred_element_type=F32)


def nt(a, b):
    return lax.dot_general(a, b, (((1,), (1,)), ((), ())), preferred_element_type=F32)


def iota(shape, dim):
    return lax.broadcasted_iota(jnp.int32, shape, dim)


def onehot(cond):
    return jnp.where(cond, 1.0, 0.0).astype(BF)


def ln(x):
    mean = jnp.mean(x, axis=-1, keepdims=True)
    centred = x - mean
    inv = lax.rsqrt(jnp.mean(centred * centred, axis=-1, keepdims=True) + LN_EPS)
    return centred * inv, inv


def ln_back(scaled, inv, grad):
    mean_grad = jnp.mean(grad, axis=-1, keepdims=True)
    mean_proj = jnp.mean(grad * scaled, axis=-1, keepdims=True)
    return inv * (grad - mean_grad - scaled * mean_proj)


def gelu_pair(v):
    gauss = jnp.exp(-0.5 * v * v)
    t = 1.0 / (1.0 + (0.3275911 * 0.7071067811865476) * jnp.abs(v))
    poly = t * (
        0.127414796 + t * (-0.142248368 + t * (0.7107068705 + t * (-0.7265760135 + t * 0.5307027145)))
    )
    tail = poly * gauss
    phi = jnp.where(v < 0.0, tail, 1.0 - tail)
    return v * phi, phi + v * gauss * 0.3989422804014327


def key_target(lanes, width, shape, dim):
    y = iota(shape, dim)
    pos = y & 15
    col = jnp.where(pos < 8, pos, pos - 2)
    valid = ((pos & 7) < 6) & (y < lanes)
    return jnp.where(valid, (y >> 4) * REACH + col + (WLON - 1), -1)


def kernel(
    x_ref, ct_ref, wqkv_ref, wproj_ref, wup_ref, wdown_ref, eb_ref,
    res_ref, gin_ref, oqkv_ref, oproj_ref, oup_ref, odown_ref, obias_ref,
    win_ref, n1_ref, sc1_ref, inv1_ref, qkv_ref, p1_ref, p2_ref, mix_ref, sc2_ref, inv2_ref, n2_ref,
    act_ref, slope_ref, gpre_ref, gqkv_ref, ghb_ref, g_ref,
    t_ref, bias1_ref, bias2_ref, ds1_ref, ds2_ref,
    perm_ref, sel_ref,
    xs_ref, xr_ref,
    strip_ref, r1_ref, s2_ref, r2_ref, s3_ref, r3_ref,
    bs_ref, br_ref, ball_ref,
    x_send, x_recv, s1_send, s1_recv, s2_send, s2_recv, s3_send, s3_recv, b_send, b_recv, bg_send, bg_recv,
):
    lat = lax.axis_index("lat")
    lon = lax.axis_index("lon")

    def at_lat(k):
        return lax.rem(lat + k + NLAT, NLAT)

    def at_lon(k):
        return lax.rem(lon + k + NLON, NLON)

    barrier = pltpu.get_barrier_semaphore()

    def greet_lat(k, carry):
        pl.semaphore_signal(barrier, inc=1, device_id={"lat": at_lat(k)}, device_id_type=MESH)
        return carry

    def greet_lon(k, carry):
        pl.semaphore_signal(barrier, inc=1, device_id={"lon": at_lon(k)}, device_id_type=MESH)
        return carry

    lax.fori_loop(1, NLAT, greet_lat, 0)
    lax.fori_loop(1, NLON, greet_lon, 0)
    for k in (-1, 1):
        pl.semaphore_signal(
            barrier, inc=1, device_id={"lat": at_lat(k), "lon": at_lon(k)}, device_id_type=MESH
        )

    lane = iota((1, C), 1) >> 5
    hm = [onehot(lane == h) for h in range(HEADS)]
    eye = onehot(iota((C, C), 0) == iota((C, C), 1))
    tgt1 = key_target(TOK, 256, (1, 256), 1)
    tgt2 = key_target(96, 128, (1, 128), 1)

    def load_window(src):
        for z in range(ZONES):
            v = src[z // 6, z % 6].astype(F32)
            win_ref[16 * z:16 * z + 16, :] = jnp.zeros((16, C), F32)
            win_ref[16 * z:16 * z + 6, :] = v[0:6]
            win_ref[16 * z + 8:16 * z + 14, :] = v[6:12]
        return win_ref[...]

    def store_window(dst, val):
        for z in range(ZONES):
            win_ref[16 * z:16 * z + 8, :] = val[16 * z:16 * z + 8]
            win_ref[16 * z + 6:16 * z + 14, :] = val[16 * z + 8:16 * z + 16]
            dst[z // 6, z % 6] = win_ref[16 * z:16 * z + 12, :].astype(BF)

    def group(val, lev, row, half):
        at = 96 * lev + 16 * row + 8 * half
        return val[at:at + 8]

    def strip(val, row0, half):
        return jnp.concatenate(
            [group(val, lev, row0 + r, half) for lev in range(2) for r in range(3)], axis=0
        ).astype(BF)

    def exchange_copies(idx):
        step = -1 if idx < 2 else 1
        targets = (
            {"lon": at_lon(step)},
            {"lat": at_lat(step)},
            {"lat": at_lat(step), "lon": at_lon(step)},
        )
        return [
            pltpu.make_async_remote_copy(
                src_ref=xs_ref.at[idx, i],
                dst_ref=xr_ref.at[idx, i],
                send_sem=x_send.at[idx, i],
                recv_sem=x_recv.at[idx, i],
                device_id=targets[i],
                device_id_type=MESH,
            )
            for i in range(3)
        ]

    def exchange_start(idx, val):
        if idx < 2:
            parts = (strip(val, 3, 0), strip(val, 0, 1), strip(val, 0, 0))
        else:
            parts = (strip(val, 0, 1), strip(val, 3, 0), strip(val, 3, 1))
        for i, copy in enumerate(exchange_copies(idx)):
            xs_ref[idx, i] = parts[i]
            copy.start()

    def exchange_finish(idx, val):
        for copy in exchange_copies(idx):
            copy.wait()
        got = [xr_ref[idx, i].astype(F32) for i in range(3)]
        row_near = 0 if idx < 2 else 3
        half_near = 0 if idx < 2 else 1
        rows = []
        for lev in range(2):
            old = 1 - lev
            for row in range(6):
                near_row = (row < 3) == (row_near == 0)
                r = row % 3
                pieces = []
                for half in range(2):
                    near_half = half == half_near
                    at = 24 * old + 8 * r
                    if near_row and near_half:
                        piece = group(val, old, (3 if idx < 2 else 0) + r, 1 - half)
                    elif near_row:
                        piece = got[0][at:at + 8]
                    elif near_half:
                        piece = got[1][at:at + 8]
                    else:
                        piece = got[2][at:at + 8]
                    pieces.append(piece)
                rows += pieces
        return jnp.concatenate(rows, axis=0)

    def load_table(b):
        t_ref[...] = jnp.zeros_like(t_ref)
        for a in range(ZONES):
            t_ref[8 * a:8 * a + 6, 0:TAB] = eb_ref[b, :, TAB * a:TAB * a + TAB]

    def split3(v):
        hi = v.astype(BF)
        rest = v - hi.astype(F32)
        mid = rest.astype(BF)
        return hi, mid, (rest - mid.astype(F32)).astype(BF)

    def expand_bias(b):
        load_table(b)
        table = t_ref[...]
        if b == 0:
            spread = [onehot(iota((384, 256), 0) == tgt1)]
            mask = jnp.broadcast_to(jnp.where(tgt1 < 0, NEG_FILL, 0.0), (96, 256))
        else:
            spread = [onehot(iota((384, 128), 0) == jnp.where(tgt2 < 0, -1, tgt2 + 138 * lv)) for lv in range(2)]
            zone = iota((96, 1), 0) >> 3
            zone = jnp.where(zone >= 6, zone - 6, zone)
            far_row = jnp.where(zone >= 3, 1, 0)
            far_key = jnp.where(iota((1, 128), 1) >= 48, 1, 0)
            last = jnp.where(lat == NLAT - 1, 1, 0)
            cut = (far_row + far_key) * last == 1
            mask = jnp.where(cut | (tgt2 < 0), NEG_FILL, 0.0)
        for c in range(WLON):
            rolled = pltpu.roll(table, c, 1) if c else table
            parts = split3(rolled)
            if b == 0:
                full = sum(nn(p, spread[0]) for p in parts) + mask
                for t in range(2):
                    bias1_ref[t, pl.ds(QPOS[c], 96, stride=16), :] = full[:, 128 * t:128 * t + 128]
            else:
                full = jnp.concatenate(
                    [sum(nn(p[48 * lv:48 * lv + 48], spread[lv]) for p in parts) for lv in range(2)], axis=0
                )
                bias2_ref[pl.ds(QPOS[c], 96, stride=16), :] = full + mask
        for p in PAD_POS:
            if b == 0:
                for t in range(2):
                    bias1_ref[t, pl.ds(p, 96, stride=16), :] = mask[:, 128 * t:128 * t + 128]
            else:
                bias2_ref[pl.ds(p, 96, stride=16), :] = mask

    def head_rows(ref, h, first, last):
        return jnp.concatenate(
            [ref[(8 * a + h) * 16:(8 * a + h) * 16 + 16, :] for a in range(first, last)], axis=0
        )

    def head_bias(b, h, seg):
        if b == 0:
            return jnp.concatenate(
                [head_rows(bias1_ref.at[0], h, 0, ZONES), head_rows(bias1_ref.at[1], h, 0, ZONES)[:, :64]], axis=1
            )
        return head_rows(bias2_ref, h, 6 * seg, 6 * seg + 6)[:, :96]

    segments = ((0, TOK),), ((0, 96), (96, 96))

    def forward(b, u):
        sc1, inv1 = ln(u)
        n1 = sc1.astype(BF)
        n1_ref[b] = n1
        sc1_ref[b] = sc1
        inv1_ref[b] = inv1
        qkv_ref[b] = nn(n1, wqkv_ref[b]).astype(BF)
        for seg, (start, size) in enumerate(segments[b]):
            q = qkv_ref[b, start:start + size, 0:C]
            k = qkv_ref[b, start:start + size, C:2 * C]
            v = qkv_ref[b, start:start + size, 2 * C:3 * C]
            mixed = jnp.zeros((size, C), F32)
            for h in range(HEADS):
                scores = nt(q * hm[h], k) * SCALE + head_bias(b, h, seg)
                top = jnp.max(scores, axis=-1, keepdims=True)
                e = jnp.exp(scores - top)
                probs = (e * (1.0 / jnp.sum(e, axis=-1, keepdims=True))).astype(BF)
                if b == 0:
                    p1_ref[h] = probs
                else:
                    p2_ref[h, start:start + size, :] = probs
                mixed = mixed + nn(probs, v * hm[h])
            mix_ref[b, start:start + size, :] = mixed.astype(BF)
        hidden = (u + nn(mix_ref[b], wproj_ref[b])).astype(BF).astype(F32)
        sc2, inv2 = ln(hidden)
        n2 = sc2.astype(BF)
        sc2_ref[b] = sc2
        inv2_ref[b] = inv2
        n2_ref[b] = n2
        acc = hidden
        for c in range(0, HID, 256):
            act, slope = gelu_pair(nn(n2, wup_ref[b, :, c:c + 256]))
            act = act.astype(BF)
            act_ref[b, :, c:c + 256] = act
            slope_ref[b, :, c:c + 256] = slope.astype(BF)
            acc = acc + nn(act, wdown_ref[b, c:c + 256, :])
        return acc.astype(BF).astype(F32)

    def backward_mlp(b, gf):
        g = gf.astype(BF)
        g_ref[b] = g
        gn2 = jnp.zeros((TOK, C), F32)
        for c in range(0, HID, 256):
            gact = nt(g, wdown_ref[b, c:c + 256, :])
            gpre = (gact * slope_ref[b, :, c:c + 256].astype(F32)).astype(BF)
            gpre_ref[b, :, c:c + 256] = gpre
            gn2 = gn2 + nt(gpre, wup_ref[b, :, c:c + 256])
        ghid = gf + ln_back(sc2_ref[b], inv2_ref[b], gn2)
        ghb_ref[b] = ghid.astype(BF)
        return ghid

    def backward_attention(b, ghid):
        gmix_all = nt(ghb_ref[b], wproj_ref[b]).astype(BF)
        for seg, (start, size) in enumerate(segments[b]):
            rows = slice(start, start + size)
            q = qkv_ref[b, rows, 0:C]
            k = qkv_ref[b, rows, C:2 * C]
            v = qkv_ref[b, rows, 2 * C:3 * C]
            gmix = gmix_all[rows]
            qt = nt(eye, q).astype(BF)
            gmt = nt(eye, gmix).astype(BF)
            gq = jnp.zeros((size, C), F32)
            gkt = []
            gvt = []
            for h in range(HEADS):
                pb = p1_ref[h] if b == 0 else p2_ref[h, rows, :]
                pf = pb.astype(F32)
                gp = nt(gmix * hm[h], v)
                ds = pf * (gp - jnp.sum(gp * pf, axis=-1, keepdims=True))
                if b == 0:
                    for a in range(ZONES):
                        at = (8 * a + h) * 16
                        ds1_ref[0, at:at + 16, :] = ds[16 * a:16 * a + 16, 0:128]
                        ds1_ref[1, at:at + 16, 0:64] = ds[16 * a:16 * a + 16, 128:192]
                else:
                    for a in range(6):
                        at = (8 * (a + 6 * seg) + h) * 16
                        ds2_ref[at:at + 16, 0:96] = ds[16 * a:16 * a + 16, :]
                dsb = ds.astype(BF)
                gq = gq + nn(dsb, k * hm[h])
                gkt.append(nn(qt[32 * h:32 * h + 32], dsb))
                gvt.append(nn(gmt[32 * h:32 * h + 32], pb))
            small = eye if size == C else eye[0:size, 0:size]
            gk = nt(small, (jnp.concatenate(gkt, axis=0) * SCALE).astype(BF)).astype(BF)
            gv = nt(small, jnp.concatenate(gvt, axis=0).astype(BF)).astype(BF)
            gqkv_ref[b, rows, 0:C] = (gq * SCALE).astype(BF)
            gqkv_ref[b, rows, C:2 * C] = gk
            gqkv_ref[b, rows, 2 * C:3 * C] = gv
        gn1 = nt(gqkv_ref[b], wqkv_ref[b])
        return (ghid + ln_back(sc1_ref[b], inv1_ref[b], gn1)).astype(BF).astype(F32)

    def put_strips(b, t, s, val):
        val = (val * NORM).astype(BF)
        for i in range(val.shape[1] // 128):
            strip_ref[b, t, s + i] = val[:, 128 * i:128 * i + 128]

    def grads_mlp(b):
        actt = nt(perm_ref[...], act_ref[b]).astype(BF)
        g = g_ref[b]
        for pair in range(2):
            at = 384 * pair
            both = [nn(actt[at + 192 * i:at + 192 * i + 192], g) for i in range(2)]
            put_strips(b, 0, 3 * pair, jnp.concatenate(both, axis=1))
        n2t = nt(eye, n2_ref[b]).astype(BF)
        for s in range(3):
            put_strips(b, 1, 2 * s, nn(n2t, gpre_ref[b, :, 256 * s:256 * s + 256]))

    def grads_attention(b):
        n1t = nt(eye, n1_ref[b]).astype(BF)
        mixt = nt(eye, mix_ref[b]).astype(BF)
        put_strips(b, 2, 0, nn(n1t, gqkv_ref[b, :, 0:256]))
        put_strips(b, 2, 2, nn(n1t, gqkv_ref[b, :, 256:512]))
        rest = [nn(n1t, gqkv_ref[b, :, 512:576]), nn(mixt, ghb_ref[b])]
        put_strips(b, 2, 4, jnp.concatenate(rest, axis=1))

    def place(b):
        return lat if b == 0 else NLAT - 1 - lat

    def owner(b, t, s):
        at = (2 * s, 2 * s + 1, (12 + 2 * s) % NLAT)[t]
        return at if b == 0 else NLAT - 1 - at

    def owned(b, t):
        at = place(b)
        if t == 0:
            return (lax.rem(at, 2) == 0) & (at < 12), at // 2
        if t == 1:
            return (lax.rem(at, 2) == 1) & (at < 12), at // 2
        back = lax.rem(at + 4, NLAT)
        return (lax.rem(back, 2) == 0) & (back < 12), back // 2

    def s1_copy(b, t, s):
        return pltpu.make_async_remote_copy(
            src_ref=strip_ref.at[b, t, s],
            dst_ref=r1_ref.at[b, t, lat],
            send_sem=s1_send.at[b, t, s],
            recv_sem=s1_recv.at[b, t],
            device_id={"lat": owner(b, t, s)},
            device_id_type=MESH,
        )

    def stage1_send(b, t):
        for s in range(6):
            @pl.when(lat != owner(b, t, s))
            def _():
                s1_copy(b, t, s).start()

            @pl.when(lat == owner(b, t, s))
            def _():
                r1_ref[b, t, lat] = strip_ref[b, t, s]

    def stage1_sent(b, t):
        for s in range(6):
            @pl.when(lat != owner(b, t, s))
            def _():
                s1_copy(b, t, s).wait_send()

    def wait_bytes(ref, sem):
        pltpu.make_async_copy(ref, ref, sem).wait()

    def stage1_reduce(b, t):
        mine, _ = owned(b, t)

        @pl.when(mine)
        def _():
            wait_bytes(r1_ref.at[b, t, pl.ds(0, NLAT - 1)], s1_recv.at[b, t])
            acc = r1_ref[b, t, 0].astype(F32)
            for i in range(1, NLAT):
                acc = acc + r1_ref[b, t, i].astype(F32)
            spread = nn(sel_ref[...], acc.astype(BF)).astype(BF)
            for j in range(NLON):
                s2_ref[b, t, j] = spread[16 * j:16 * j + 16]
            r2_ref[b, t, lon] = s2_ref[b, t, lon]

            def send(k, carry):
                to = at_lon(k)
                pltpu.make_async_remote_copy(
                    src_ref=s2_ref.at[b, t, to],
                    dst_ref=r2_ref.at[b, t, lon],
                    send_sem=s2_send.at[b, t],
                    recv_sem=s2_recv.at[b, t],
                    device_id={"lon": to},
                    device_id_type=MESH,
                ).start()
                return carry

            lax.fori_loop(1, NLON, send, 0)

    def stage2_reduce(b, t):
        mine, which = owned(b, t)

        @pl.when(mine)
        def _():
            wait_bytes(r2_ref.at[b, t, pl.ds(0, NLON - 1)], s2_recv.at[b, t])
            acc = r2_ref[b, t, 0].astype(F32)
            for i in range(1, NLON):
                acc = acc + r2_ref[b, t, i].astype(F32)
            total = acc.astype(BF)
            s3_ref[b, t] = total
            r3_ref[b, t, which] = total

            def send(k, carry):
                pltpu.make_async_remote_copy(
                    src_ref=s3_ref.at[b, t],
                    dst_ref=r3_ref.at[b, t, which],
                    send_sem=s3_send.at[b, t],
                    recv_sem=s3_recv.at[b, t],
                    device_id={"lat": at_lat(k)},
                    device_id_type=MESH,
                ).start()
                return carry

            lax.fori_loop(1, NLAT, send, 0)

    def stage3_finish(b, t):
        mine, _ = owned(b, t)

        @pl.when(mine)
        def _():
            wait_bytes(r3_ref.at[b, t, pl.ds(0, 5)], s3_recv.at[b, t])

        @pl.when(jnp.logical_not(mine))
        def _():
            wait_bytes(r3_ref.at[b, t], s3_recv.at[b, t])

        full = jnp.concatenate([r3_ref[b, t, s].astype(F32)[0:8] for s in range(6)], axis=1)
        if t == 0:
            for s in range(4):
                part = full[:, 192 * s:192 * s + 192]
                for i in range(SHARD):
                    odown_ref[b, 4 * i + s:4 * i + s + 1, :] = part[i:i + 1]
        elif t == 1:
            oup_ref[b] = full[0:SHARD]
        else:
            oqkv_ref[b] = full[0:SHARD, 0:576]
            oproj_ref[b] = full[0:SHARD, 576:768]

    def stages_sent(b, t):
        mine, _ = owned(b, t)
        stage1_sent(b, t)

        @pl.when(mine)
        def _():
            wait_bytes(s2_ref.at[b, t, pl.ds(0, NLON - 1)], s2_send.at[b, t])
            wait_bytes(s2_ref.at[b, t, pl.ds(0, NLAT - 1)], s3_send.at[b, t])

    tiles = (18, 12)
    tile0 = (0, 18)

    def fold_bias(b):
        total = None
        for c in range(WLON):
            if b == 0:
                spread = [onehot(iota((128, 384), 1) == key_target(TOK, 256, (256, 1), 0)[128 * t:128 * t + 128]) for t in range(2)]
                got = [ds1_ref[t, pl.ds(QPOS[c], 96, stride=16), :].astype(BF) for t in range(2)]
                part = nn(got[0], spread[0]) + nn(got[1][:, 0:64], spread[1][0:64])
            else:
                spread = [onehot(iota((128, 256), 1) == key_target(96, 128, (128, 1), 0))]
                got = ds2_ref[pl.ds(QPOS[c], 96, stride=16), :].astype(BF)
                part = nn(got[:, 0:96], spread[0][0:96])
            width = part.shape[1]
            if c:
                part = pltpu.roll(part, width - c, 1)
            total = part if total is None else total + part
        total = total.astype(BF)
        lanes = total.shape[1] // 128
        for rt in range(6):
            for lt in range(lanes):
                bs_ref[tile0[b] + rt * lanes + lt] = total[16 * rt:16 * rt + 16, 128 * lt:128 * lt + 128]

    def b_copy(b, i):
        return pltpu.make_async_remote_copy(
            src_ref=bs_ref.at[i],
            dst_ref=br_ref.at[lon],
            send_sem=b_send.at[i],
            recv_sem=b_recv,
            device_id={"lon": i},
            device_id_type=MESH,
        )

    def bias_send(b):
        for i in range(tile0[b], tile0[b] + tiles[b]):
            @pl.when(lon != i)
            def _():
                b_copy(b, i).start()

            @pl.when(lon == i)
            def _():
                br_ref[lon] = bs_ref[i]

    def bias_mine(b):
        return (lon >= tile0[b]) & (lon < tile0[b] + tiles[b])

    def bias_reduce(b):
        @pl.when(bias_mine(b))
        def _():
            wait_bytes(br_ref.at[pl.ds(0, NLON - 1)], b_recv)
            acc = br_ref[0].astype(F32)
            for i in range(1, NLON):
                acc = acc + br_ref[i].astype(F32)
            ball_ref[lon] = acc.astype(BF)

            def send(k, carry):
                pltpu.make_async_remote_copy(
                    src_ref=ball_ref.at[lon],
                    dst_ref=ball_ref.at[lon],
                    send_sem=bg_send,
                    recv_sem=bg_recv.at[b],
                    device_id={"lon": at_lon(k)},
                    device_id_type=MESH,
                ).start()
                return carry

            lax.fori_loop(1, NLON, send, 0)

    def bias_finish(b):
        mine = bias_mine(b)

        @pl.when(mine)
        def _():
            wait_bytes(ball_ref.at[pl.ds(tile0[b], tiles[b] - 1)], bg_recv.at[b])

        @pl.when(jnp.logical_not(mine))
        def _():
            wait_bytes(ball_ref.at[pl.ds(tile0[b], tiles[b])], bg_recv.at[b])

        lanes = 3 if b == 0 else 2
        for a in range(ZONES):
            row = jnp.concatenate(
                [
                    ball_ref[tile0[b] + (a // 2) * lanes + lt].astype(F32)[8 * (a % 2):8 * (a % 2) + 6]
                    for lt in range(lanes)
                ],
                axis=1,
            )
            if b == 0:
                obias_ref[b, :, TAB * a:TAB * a + TAB] = row[:, 0:TAB]
            else:
                half = row[:, 0:138]
                zero = jnp.zeros((6, 138), F32)
                both = [half, zero] if a < 6 else [zero, half]
                obias_ref[b, :, TAB * a:TAB * a + TAB] = jnp.concatenate(both, axis=1)

    def bias_sent(b):
        for i in range(tile0[b], tile0[b] + tiles[b]):
            @pl.when(lon != i)
            def _():
                b_copy(b, i).wait_send()

        @pl.when(bias_mine(b))
        def _():
            wait_bytes(br_ref.at[pl.ds(0, NLON - 1)], bg_send)

    expand_bias(0)
    u1 = load_window(x_ref)
    out1 = forward(0, u1)
    pl.semaphore_wait(barrier, NLAT - 1 + NLON - 1 + 2)
    exchange_start(1, out1)
    ct = load_window(ct_ref)
    exchange_start(0, ct)
    expand_bias(1)
    for s in range(4):
        perm_ref[192 * s:192 * s + 192, :] = onehot(iota((192, HID), 1) == 4 * iota((192, HID), 0) + s)
    row = iota((512, 1), 0)
    pos = row & 15
    sel_ref[...] = onehot(iota((512, C), 1) == jnp.where(pos < SHARD, (row >> 4) * SHARD + pos, -1))
    u2 = exchange_finish(1, out1)
    out2 = forward(1, u2)
    exchange_start(2, out2)
    g2 = exchange_finish(0, ct)
    ghid2 = backward_mlp(1, g2)
    gsec = backward_attention(1, ghid2)
    exchange_start(3, gsec)
    grads_mlp(1)
    grads_attention(1)
    for t in range(3):
        stage1_send(1, t)
    fold_bias(1)
    bias_send(1)
    store_window(res_ref, exchange_finish(2, out2))
    g1 = exchange_finish(3, gsec)
    ghid1 = backward_mlp(0, g1)
    grads_mlp(0)
    stage1_send(0, 0)
    stage1_send(0, 1)
    for t in range(3):
        stage1_reduce(1, t)
    bias_reduce(1)
    gin = backward_attention(0, ghid1)
    grads_attention(0)
    stage1_send(0, 2)
    fold_bias(0)
    bias_send(0)
    stage1_reduce(0, 0)
    stage1_reduce(0, 1)
    for t in range(3):
        stage2_reduce(1, t)
    store_window(gin_ref, gin)
    bias_finish(1)
    stage1_reduce(0, 2)
    bias_reduce(0)
    for t in range(3):
        stage3_finish(1, t)
    stage2_reduce(0, 0)
    stage2_reduce(0, 1)
    stage2_reduce(0, 2)
    bias_finish(0)
    for t in range(3):
        stage3_finish(0, t)
    for b in range(2):
        for t in range(3):
            stages_sent(b, t)
        bias_sent(b)


def on_device(inputs, cotangent, w_qkv, w_proj, w_up, w_down, earth_bias):
    vm = pl.BlockSpec(memory_space=pltpu.VMEM)
    outs = pl.pallas_call(
        kernel,
        out_shape=(
            jax.ShapeDtypeStruct((2, 6, 12, C), BF),
            jax.ShapeDtypeStruct((2, 6, 12, C), BF),
            jax.ShapeDtypeStruct((2, SHARD, 576), F32),
            jax.ShapeDtypeStruct((2, SHARD, 192), F32),
            jax.ShapeDtypeStruct((2, SHARD, 768), F32),
            jax.ShapeDtypeStruct((2, 24, 192), F32),
            jax.ShapeDtypeStruct((2, HEADS, 3312), F32),
        ),
        in_specs=[vm] * 7,
        out_specs=(vm,) * 7,
        scratch_shapes=[
            pltpu.VMEM((TOK, C), F32),
            pltpu.VMEM((2, TOK, C), BF),
            pltpu.VMEM((2, TOK, C), F32),
            pltpu.VMEM((2, TOK, 1), F32),
            pltpu.VMEM((2, TOK, 576), BF),
            pltpu.VMEM((HEADS, TOK, TOK), BF),
            pltpu.VMEM((HEADS, TOK, 96), BF),
            pltpu.VMEM((2, TOK, C), BF),
            pltpu.VMEM((2, TOK, C), F32),
            pltpu.VMEM((2, TOK, 1), F32),
            pltpu.VMEM((2, TOK, C), BF),
            pltpu.VMEM((2, TOK, HID), BF),
            pltpu.VMEM((2, TOK, HID), BF),
            pltpu.VMEM((2, TOK, HID), BF),
            pltpu.VMEM((2, TOK, 576), BF),
            pltpu.VMEM((2, TOK, C), BF),
            pltpu.VMEM((2, TOK, C), BF),
            pltpu.VMEM((96, 384), F32),
            pltpu.VMEM((2, 1536, 128), F32),
            pltpu.VMEM((1536, 128), F32),
            pltpu.VMEM((2, 1536, 128), F32),
            pltpu.VMEM((1536, 128), F32),
            pltpu.VMEM((HID, HID), BF),
            pltpu.VMEM((512, C), BF),
            pltpu.VMEM((4, 3, 48, C), BF),
            pltpu.VMEM((4, 3, 48, C), BF),
            pltpu.VMEM((2, 3, 6, C, 128), BF),
            pltpu.VMEM((2, 3, NLAT, C, 128), BF),
            pltpu.VMEM((2, 3, NLON, 16, 128), BF),
            pltpu.VMEM((2, 3, NLON, 16, 128), BF),
            pltpu.VMEM((2, 3, 16, 128), BF),
            pltpu.VMEM((2, 3, 6, 16, 128), BF),
            pltpu.VMEM((30, 16, 128), BF),
            pltpu.VMEM((NLON, 16, 128), BF),
            pltpu.VMEM((NLON, 16, 128), BF),
            pltpu.SemaphoreType.DMA((4, 3)),
            pltpu.SemaphoreType.DMA((4, 3)),
            pltpu.SemaphoreType.DMA((2, 3, 6)),
            pltpu.SemaphoreType.DMA((2, 3)),
            pltpu.SemaphoreType.DMA((2, 3)),
            pltpu.SemaphoreType.DMA((2, 3)),
            pltpu.SemaphoreType.DMA((2, 3)),
            pltpu.SemaphoreType.DMA((2, 3)),
            pltpu.SemaphoreType.DMA((30,)),
            pltpu.SemaphoreType.DMA,
            pltpu.SemaphoreType.DMA,
            pltpu.SemaphoreType.DMA((2,)),
        ],
        compiler_params=pltpu.CompilerParams(
            collective_id=0, has_side_effects=True, vmem_limit_bytes=50 * 1024 * 1024
        ),
        name="earth_blocks",
    )(inputs, cotangent, w_qkv, w_proj, w_up, w_down, earth_bias.reshape(2, HEADS, 3312))
    result, grad_inputs, g_qkv, g_proj, g_up, g_down, g_bias = outs
    return result, grad_inputs, g_qkv, g_proj, g_up, g_down, g_bias.reshape(2, 1, 1, HEADS, 3312)


def solution(mesh):
    field = P(None, "lat", "lon", None)
    shard = P(None, "lon", None)
    bias = P(None, "lat", None, None, None)
    return jax.shard_map(
        on_device,
        mesh=mesh,
        in_specs=(field, field, P(), P(), P(), P(), bias),
        out_specs=(field, field, shard, shard, shard, shard, bias),
        check_vma=False,
    )
```

```python
import jax
import jax.numpy as jnp
from jax import lax
from jax.experimental import pallas as pl
from jax.experimental.pallas import tpu as pltpu
from jax.sharding import PartitionSpec as P

BF = jnp.bfloat16
F32 = jnp.float32
MESH = pl.DeviceIdType.MESH

HEADS = 6
C = 192
HID = 768
WLON = 12
ZONES = 12
REACH = 23
TAB = ZONES * REACH
NLAT = 16
NLON = 32
RING = 16
CHIPS = 8
SHARD = 6
TOK = 192
NEG_FILL = -1e30
LN_EPS = 1e-05
SCALE = 32.0 ** -0.5
NORM = 73728.0 ** -0.5

QPOS = [c if c < 6 else c + 2 for c in range(WLON)]
PAD_POS = [6, 7, 14, 15]


def nn(a, b):
    return lax.dot_general(a, b, (((1,), (0,)), ((), ())), preferred_element_type=F32)


def nt(a, b):
    return lax.dot_general(a, b, (((1,), (1,)), ((), ())), preferred_element_type=F32)


def iota(shape, dim):
    return lax.broadcasted_iota(jnp.int32, shape, dim)


def onehot(cond):
    return jnp.where(cond, 1.0, 0.0).astype(BF)


def ln(x):
    mean = jnp.mean(x, axis=-1, keepdims=True)
    centred = x - mean
    inv = lax.rsqrt(jnp.mean(centred * centred, axis=-1, keepdims=True) + LN_EPS)
    return centred * inv, inv


def ln_back(scaled, inv, grad):
    mean_grad = jnp.mean(grad, axis=-1, keepdims=True)
    mean_proj = jnp.mean(grad * scaled, axis=-1, keepdims=True)
    return inv * (grad - mean_grad - scaled * mean_proj)


def gelu_pair(v):
    gauss = jnp.exp(-0.5 * v * v)
    t = 1.0 / (1.0 + (0.3275911 * 0.7071067811865476) * jnp.abs(v))
    poly = t * (
        0.127414796 + t * (-0.142248368 + t * (0.7107068705 + t * (-0.7265760135 + t * 0.5307027145)))
    )
    tail = poly * gauss
    phi = jnp.where(v < 0.0, tail, 1.0 - tail)
    return v * phi, phi + v * gauss * 0.3989422804014327


def key_target(lanes, width, shape, dim):
    y = iota(shape, dim)
    pos = y & 15
    col = jnp.where(pos < 8, pos, pos - 2)
    valid = ((pos & 7) < 6) & (y < lanes)
    return jnp.where(valid, (y >> 4) * REACH + col + (WLON - 1), -1)


def kernel(
    x_ref, ct_hbm, wqkv_hbm, wproj_hbm, wup_hbm, wdown_hbm, eb_ref,
    res_ref, gin_ref, oqkv_ref, oproj_ref, oup_ref, odown_ref, obias_ref,
    ct_ref, wqkv_ref, wproj_ref, wup_ref, wdown_ref, in_sem, win_ref, n1_ref, sc1_ref, inv1_ref, qkv_ref, p1_ref, p2_ref, mix_ref, sc2_ref, inv2_ref, n2_ref,
    act_ref, slope_ref, gpre_ref, gqkv_ref, ghb_ref, g_ref,
    t_ref, bias1_ref, bias2_ref, ds1_ref, ds2_ref,
    perm_ref, sel_ref,
    xs_ref, xr_ref,
    strip_ref, r0_ref, a_du_ref, a_qp_ref, r1_du_ref, r1_qp_ref, s2_ref, r2_ref, s3_ref, r3_ref,
    bs_ref, br_ref, ball_ref,
    x_send, x_recv, s0_send, s0_recv, s1_send, s1_recv, s2_send, s2_recv, s3_send, s3_recv,
    b_send, b_recv, bg_send, bg_recv,
):
    lat = lax.axis_index("lat")
    lon = lax.axis_index("lon")

    def at_lat(k):
        return lax.rem(lat + k + NLAT, NLAT)

    def at_lon(k):
        return lax.rem(lon + k + NLON, NLON)

    loads = [
        pltpu.make_async_copy(src, dst, in_sem.at[i])
        for i, (src, dst) in enumerate(
            (
                (wqkv_hbm, wqkv_ref),
                (wproj_hbm, wproj_ref),
                (wup_hbm, wup_ref),
                (wdown_hbm, wdown_ref),
                (ct_hbm, ct_ref),
            )
        )
    ]
    for load in loads:
        load.start()

    barrier = pltpu.get_barrier_semaphore()

    def greet_lat(k, carry):
        pl.semaphore_signal(barrier, inc=1, device_id={"lat": at_lat(k)}, device_id_type=MESH)
        return carry

    def greet_lon(k, carry):
        pl.semaphore_signal(barrier, inc=1, device_id={"lon": at_lon(k)}, device_id_type=MESH)
        return carry

    lax.fori_loop(1, NLAT, greet_lat, 0)
    lax.fori_loop(1, NLON, greet_lon, 0)
    def greet_far(k, carry):
        to = {"lat": lax.rem(lat + 2 * k, NLAT), "lon": lax.rem(lon + RING, NLON)}
        pl.semaphore_signal(barrier, inc=1, device_id=to, device_id_type=MESH)
        return carry

    lax.fori_loop(1, CHIPS, greet_far, 0)
    for k in (-1, 1):
        pl.semaphore_signal(
            barrier, inc=1, device_id={"lat": at_lat(k), "lon": at_lon(k)}, device_id_type=MESH
        )

    lane = iota((1, C), 1) >> 5
    hm = [onehot(lane == h) for h in range(HEADS)]
    eye = onehot(iota((C, C), 0) == iota((C, C), 1))
    tgt1 = key_target(TOK, 256, (1, 256), 1)
    tgt2 = key_target(96, 128, (1, 128), 1)

    def load_window(src):
        win_ref[...] = jnp.zeros((TOK, C), F32)
        for r in range(6):
            for c in range(WLON):
                v = src[r, c].astype(F32)
                for lev in range(2):
                    at = 96 * lev + 16 * r + QPOS[c]
                    win_ref[at:at + 1, :] = v[lev:lev + 1]
        return win_ref[...]

    def store_window(dst, val):
        for r in range(6):
            for c in range(WLON):
                at = 16 * r + QPOS[c]
                dst[r, c] = jnp.concatenate([val[at:at + 1], val[at + 96:at + 97]], axis=0).astype(BF)

    def group(val, lev, row, half):
        at = 96 * lev + 16 * row + 8 * half
        return val[at:at + 8]

    def strip(val, row0, half):
        return jnp.concatenate(
            [group(val, lev, row0 + r, half) for lev in range(2) for r in range(3)], axis=0
        ).astype(BF)

    def exchange_copies(idx):
        step = -1 if idx < 2 else 1
        targets = (
            {"lon": at_lon(step)},
            {"lat": at_lat(step)},
            {"lat": at_lat(step), "lon": at_lon(step)},
        )
        return [
            pltpu.make_async_remote_copy(
                src_ref=xs_ref.at[idx, i],
                dst_ref=xr_ref.at[idx, i],
                send_sem=x_send.at[idx, i],
                recv_sem=x_recv.at[idx, i],
                device_id=targets[i],
                device_id_type=MESH,
            )
            for i in range(3)
        ]

    def exchange_start(idx, val):
        if idx < 2:
            parts = (strip(val, 3, 0), strip(val, 0, 1), strip(val, 0, 0))
        else:
            parts = (strip(val, 0, 1), strip(val, 3, 0), strip(val, 3, 1))
        for i, copy in enumerate(exchange_copies(idx)):
            xs_ref[idx, i] = parts[i]
            copy.start()

    def exchange_finish(idx, val):
        for copy in exchange_copies(idx):
            copy.wait()
        got = [xr_ref[idx, i].astype(F32) for i in range(3)]
        row_near = 0 if idx < 2 else 3
        half_near = 0 if idx < 2 else 1
        rows = []
        for lev in range(2):
            old = 1 - lev
            for row in range(6):
                near_row = (row < 3) == (row_near == 0)
                r = row % 3
                pieces = []
                for half in range(2):
                    near_half = half == half_near
                    at = 24 * old + 8 * r
                    if near_row and near_half:
                        piece = group(val, old, (3 if idx < 2 else 0) + r, 1 - half)
                    elif near_row:
                        piece = got[0][at:at + 8]
                    elif near_half:
                        piece = got[1][at:at + 8]
                    else:
                        piece = got[2][at:at + 8]
                    pieces.append(piece)
                rows += pieces
        return jnp.concatenate(rows, axis=0)

    def load_table(b):
        t_ref[...] = jnp.zeros_like(t_ref)
        for a in range(ZONES):
            if b == 0:
                rows = pl.ds(a, HEADS, stride=ZONES)
            else:
                rows = pl.ds(36 * (a // 6) + a % 6, HEADS, stride=6)
            for lt in range(3):
                width = min(128, TAB - 128 * lt)
                lane = TAB * a + 128 * lt
                piece = eb_ref[b, :, lane:lane + width]
                if width < 128:
                    piece = jnp.concatenate([piece, jnp.zeros((HEADS, 128 - width), F32)], axis=1)
                t_ref[lt, rows, :] = piece
        return jnp.concatenate([t_ref[lt] for lt in range(3)], axis=1)

    def split3(v):
        hi = v.astype(BF)
        rest = v - hi.astype(F32)
        mid = rest.astype(BF)
        return hi, mid, (rest - mid.astype(F32)).astype(BF)

    def expand_bias(b):
        table = load_table(b)
        if b == 0:
            spread = onehot(iota((384, 256), 0) == tgt1)
            mask = jnp.broadcast_to(jnp.where(tgt1 < 0, NEG_FILL, 0.0), (72, 256))
        else:
            spread = jnp.concatenate(
                [onehot(iota((384, 128), 0) == jnp.where(tgt2 < 0, -1, tgt2 + 138 * lv)) for lv in range(2)], axis=1
            )
            row = iota((72, 1), 0)
            row = jnp.where(row >= 36, row - 36, row)
            far_row = jnp.where(lax.rem(row, 6) >= 3, 1, 0)
            far_key = jnp.where(iota((1, 128), 1) >= 48, 1, 0)
            last = jnp.where(lat == NLAT - 1, 1, 0)
            cut = (far_row + far_key) * last == 1
            mask = jnp.where(cut | (tgt2 < 0), NEG_FILL, 0.0)
            low = iota((72, 1), 0) < 36
        for c in range(WLON):
            rolled = pltpu.roll(table, c, 1) if c else table
            full = sum(nn(p, spread) for p in split3(rolled))
            if b == 0:
                full = full + mask
                for t in range(2):
                    bias1_ref[t, pl.ds(QPOS[c], 72, stride=16), :] = full[:, 128 * t:128 * t + 128]
            else:
                bias2_ref[pl.ds(QPOS[c], 72, stride=16), :] = jnp.where(low, full[:, 0:128], full[:, 128:256]) + mask
        for p in PAD_POS:
            if b == 0:
                for t in range(2):
                    bias1_ref[t, pl.ds(p, 72, stride=16), :] = mask[:, 128 * t:128 * t + 128]
            else:
                bias2_ref[pl.ds(p, 72, stride=16), :] = mask

    def head_bias(b, h, seg):
        if b == 0:
            rows = slice(TOK * h, TOK * h + TOK)
            return jnp.concatenate([bias1_ref[0, rows, :], bias1_ref[1, rows, 0:64]], axis=1)
        at = 96 * (HEADS * seg + h)
        return bias2_ref[at:at + 96, 0:96]

    segments = ((0, TOK),), ((0, 96), (96, 96))

    def forward(b, u):
        sc1, inv1 = ln(u)
        n1 = sc1.astype(BF)
        n1_ref[b] = n1
        sc1_ref[b] = sc1
        inv1_ref[b] = inv1
        qkv_ref[b] = nn(n1, wqkv_ref[b]).astype(BF)
        for seg, (start, size) in enumerate(segments[b]):
            q = qkv_ref[b, start:start + size, 0:C]
            k = qkv_ref[b, start:start + size, C:2 * C]
            v = qkv_ref[b, start:start + size, 2 * C:3 * C]
            mixed = jnp.zeros((size, C), F32)
            for h in range(HEADS):
                scores = nt(q * hm[h], k) * SCALE + head_bias(b, h, seg)
                top = jnp.max(scores, axis=-1, keepdims=True)
                e = jnp.exp(scores - top)
                probs = (e * (1.0 / jnp.sum(e, axis=-1, keepdims=True))).astype(BF)
                if b == 0:
                    p1_ref[h] = probs
                else:
                    p2_ref[h, start:start + size, :] = probs
                mixed = mixed + nn(probs, v * hm[h])
            mix_ref[b, start:start + size, :] = mixed.astype(BF)
        hidden = (u + nn(mix_ref[b], wproj_ref[b])).astype(BF).astype(F32)
        sc2, inv2 = ln(hidden)
        n2 = sc2.astype(BF)
        sc2_ref[b] = sc2
        inv2_ref[b] = inv2
        n2_ref[b] = n2
        acc = hidden
        for c in range(0, HID, 256):
            act, slope = gelu_pair(nn(n2, wup_ref[b, :, c:c + 256]))
            act = act.astype(BF)
            act_ref[b, :, c:c + 256] = act
            slope_ref[b, :, c:c + 256] = slope.astype(BF)
            acc = acc + nt(act, wdown_ref[b, :, c:c + 256])
        return acc.astype(BF).astype(F32)

    def backward_mlp(b, gf):
        g = gf.astype(BF)
        g_ref[b] = g
        gn2 = jnp.zeros((TOK, C), F32)
        for c in range(0, HID, 256):
            gact = nn(g, wdown_ref[b, :, c:c + 256])
            gpre = (gact * slope_ref[b, :, c:c + 256].astype(F32)).astype(BF)
            gpre_ref[b, :, c:c + 256] = gpre
            gn2 = gn2 + nt(gpre, wup_ref[b, :, c:c + 256])
        ghid = gf + ln_back(sc2_ref[b], inv2_ref[b], gn2)
        ghb_ref[b] = ghid.astype(BF)
        return ghid

    def attention_grads(b):
        gmix_all = nt(ghb_ref[b], wproj_ref[b]).astype(BF)
        for seg, (start, size) in enumerate(segments[b]):
            rows = slice(start, start + size)
            q = qkv_ref[b, rows, 0:C]
            k = qkv_ref[b, rows, C:2 * C]
            v = qkv_ref[b, rows, 2 * C:3 * C]
            gmix = gmix_all[rows]
            qt = nt(eye, q).astype(BF)
            gmt = nt(eye, gmix).astype(BF)
            gq = jnp.zeros((size, C), F32)
            gkt = []
            gvt = []
            for h in range(HEADS):
                pb = p1_ref[h] if b == 0 else p2_ref[h, rows, :]
                pf = pb.astype(F32)
                gp = nt(gmix * hm[h], v)
                ds = pf * (gp - jnp.sum(gp * pf, axis=-1, keepdims=True))
                if b == 0:
                    ds1_ref[0, TOK * h:TOK * h + TOK, :] = ds[:, 0:128]
                    ds1_ref[1, TOK * h:TOK * h + TOK, 0:64] = ds[:, 128:192]
                else:
                    at = 96 * (HEADS * seg + h)
                    ds2_ref[at:at + 96, 0:96] = ds
                dsb = ds.astype(BF)
                gq = gq + nn(dsb, k * hm[h])
                gkt.append(nn(qt[32 * h:32 * h + 32], dsb))
                gvt.append(nn(gmt[32 * h:32 * h + 32], pb))
            small = eye if size == C else eye[0:size, 0:size]
            gk = nt(small, (jnp.concatenate(gkt, axis=0) * SCALE).astype(BF)).astype(BF)
            gv = nt(small, jnp.concatenate(gvt, axis=0).astype(BF)).astype(BF)
            gqkv_ref[b, rows, 0:C] = (gq * SCALE).astype(BF)
            gqkv_ref[b, rows, C:2 * C] = gk
            gqkv_ref[b, rows, 2 * C:3 * C] = gv

    def input_grad(b, ghid):
        gn1 = nt(gqkv_ref[b], wqkv_ref[b])
        return (ghid + ln_back(sc1_ref[b], inv1_ref[b], gn1)).astype(BF).astype(F32)

    def put_strips(b, t, s, val):
        val = (val * NORM).astype(BF)
        for i in range(val.shape[1] // 128):
            strip_ref[b, t, s + i] = val[:, 128 * i:128 * i + 128]

    def grads_mlp(b):
        actt = nt(perm_ref[...], act_ref[b]).astype(BF)
        g = g_ref[b]
        for pair in range(2):
            at = 384 * pair
            both = [nn(actt[at + 192 * i:at + 192 * i + 192], g) for i in range(2)]
            put_strips(b, 0, 3 * pair, jnp.concatenate(both, axis=1))
        n2t = nt(eye, n2_ref[b]).astype(BF)
        for s in range(3):
            put_strips(b, 1, 2 * s, nn(n2t, gpre_ref[b, :, 256 * s:256 * s + 256]))

    def grads_attention(b):
        n1t = nt(eye, n1_ref[b]).astype(BF)
        mixt = nt(eye, mix_ref[b]).astype(BF)
        put_strips(b, 2, 0, nn(n1t, gqkv_ref[b, :, 0:256]))
        put_strips(b, 2, 2, nn(n1t, gqkv_ref[b, :, 256:512]))
        rest = [nn(n1t, gqkv_ref[b, :, 512:576]), nn(mixt, ghb_ref[b])]
        put_strips(b, 2, 4, jnp.concatenate(rest, axis=1))

    core = lax.rem(lat, 2)
    chip = lat // 2
    ring = lon // RING
    z = lax.rem(lon, RING)
    half = C // 2
    a_refs = (a_du_ref, a_qp_ref)
    r1_refs = (r1_du_ref, r1_qp_ref)

    def place(b):
        return chip if b else lax.rem(chip + 4, 8)

    def owned(b, kind):
        at = place(b)
        if kind == 0:
            return at // 3 == core, at - 3 * core
        return (at >= 6) | (at == 3 - 3 * core), jnp.where(at >= 6, at - 6, 2)

    def owner(b, kind, i):
        if kind == 0:
            at = 3 * core + i
        else:
            at = 6 + i if i < 2 else 3 - 3 * core
        at = at if b else lax.rem(at + 4, 8)
        return 2 * at + core

    def wait_bytes(ref, sem):
        pltpu.make_async_copy(ref, ref, sem).wait()

    def s0_copy(b, t):
        return pltpu.make_async_remote_copy(
            src_ref=strip_ref.at[b, t, pl.ds(3 - 3 * core, 3)],
            dst_ref=r0_ref.at[b, t],
            send_sem=s0_send.at[b, t],
            recv_sem=s0_recv.at[b, t],
            device_id={"lat": lat + 1 - 2 * core},
            device_id_type=MESH,
        )

    def stage0_send(b, t):
        s0_copy(b, t).start()

    def s1_copy(b, kind, i, g):
        return pltpu.make_async_remote_copy(
            src_ref=a_refs[kind].at[b, i, g],
            dst_ref=r1_refs[kind].at[b, CHIPS * ring + chip],
            send_sem=s1_send.at[b, kind, i, g],
            recv_sem=s1_recv.at[b, kind],
            device_id={"lat": owner(b, kind, i), "lon": RING * g + z},
            device_id_type=MESH,
        )

    def s1_here(b, kind, i, g):
        return (lat == owner(b, kind, i)) & (ring == g)

    def stage1_send(b, kind):
        groups = (0, 1) if kind == 0 else (2,)
        for t in groups:
            s0_copy(b, t).wait_recv()
        for i in range(3):
            for part, t in enumerate(groups):
                both = strip_ref[b, t, 3 * core + i].astype(F32) + r0_ref[b, t, i].astype(F32)
                for g in range(2):
                    a_refs[kind][b, i, g, part] = both[half * g:half * g + half].astype(BF)
            for g in range(2):
                here = s1_here(b, kind, i, g)

                @pl.when(jnp.logical_not(here))
                def _():
                    s1_copy(b, kind, i, g).start()

                @pl.when(here)
                def _():
                    r1_refs[kind][b, CHIPS * ring + chip] = a_refs[kind][b, i, g]

    def stage1_reduce(b, kind):
        mine, _ = owned(b, kind)
        parts = 2 if kind == 0 else 1

        @pl.when(mine)
        def _():
            ref = r1_refs[kind]
            wait_bytes(ref.at[b, pl.ds(0, 2 * CHIPS - 1)], s1_recv.at[b, kind])
            spread = []
            for part in range(parts):
                acc = ref[b, 0, part].astype(F32)
                for i in range(1, 2 * CHIPS):
                    acc = acc + ref[b, i, part].astype(F32)
                spread.append(nn(sel_ref[...], acc.astype(BF)))
            if parts == 1:
                spread.append(jnp.zeros((8 * RING, 128), F32))
            for j in range(RING):
                tile = jnp.concatenate([v[8 * j:8 * j + 8] for v in spread], axis=0)
                s2_ref[b, kind, j] = tile.astype(BF)
            r2_ref[b, kind, z] = s2_ref[b, kind, z]

            def send(k, carry):
                to = lax.rem(z + k, RING)
                pltpu.make_async_remote_copy(
                    src_ref=s2_ref.at[b, kind, to],
                    dst_ref=r2_ref.at[b, kind, z],
                    send_sem=s2_send.at[b, kind],
                    recv_sem=s2_recv.at[b, kind],
                    device_id={"lon": RING * ring + to},
                    device_id_type=MESH,
                ).start()
                return carry

            lax.fori_loop(1, RING, send, 0)

    def stage2_reduce(b, kind):
        mine, i = owned(b, kind)
        which = 3 * core + i

        @pl.when(mine)
        def _():
            wait_bytes(r2_ref.at[b, kind, pl.ds(0, RING - 1)], s2_recv.at[b, kind])
            acc = r2_ref[b, kind, 0].astype(F32)
            for j in range(1, RING):
                acc = acc + r2_ref[b, kind, j].astype(F32)
            total = acc.astype(BF)
            s3_ref[b, kind] = total
            r3_ref[b, kind, which] = total

            def send(k, carry):
                pltpu.make_async_remote_copy(
                    src_ref=s3_ref.at[b, kind],
                    dst_ref=r3_ref.at[b, kind, which],
                    send_sem=s3_send.at[b, kind],
                    recv_sem=s3_recv.at[b, kind],
                    device_id={"lat": at_lat(k)},
                    device_id_type=MESH,
                ).start()
                return carry

            lax.fori_loop(1, NLAT, send, 0)

    def put_rows(ref, b, val):
        for i in range(SHARD):
            ref[i, b:b + 1, :] = val[i:i + 1]

    def stage3_finish(b, kind):
        mine, _ = owned(b, kind)

        @pl.when(mine)
        def _():
            wait_bytes(r3_ref.at[b, kind, pl.ds(0, 5)], s3_recv.at[b, kind])

        @pl.when(jnp.logical_not(mine))
        def _():
            wait_bytes(r3_ref.at[b, kind], s3_recv.at[b, kind])

        tiles = [r3_ref[b, kind, s].astype(F32) for s in range(6)]
        first = jnp.concatenate([v[0:8] for v in tiles], axis=1)
        if kind == 0:
            for s in range(4):
                part = first[:, 192 * s:192 * s + 192]
                for i in range(SHARD):
                    odown_ref[b, 4 * i + s:4 * i + s + 1, :] = part[i:i + 1]
            put_rows(oup_ref, b, jnp.concatenate([v[8:16] for v in tiles], axis=1))
        else:
            put_rows(oqkv_ref, b, first[:, 0:576])
            put_rows(oproj_ref, b, first[:, 576:768])

    def stages_sent(b):
        for t in range(3):
            s0_copy(b, t).wait_send()
        for kind in range(2):
            for i in range(3):
                for g in range(2):
                    @pl.when(jnp.logical_not(s1_here(b, kind, i, g)))
                    def _():
                        s1_copy(b, kind, i, g).wait_send()

            @pl.when(owned(b, kind)[0])
            def _():
                wait_bytes(s2_ref.at[b, kind, pl.ds(0, RING - 1)], s2_send.at[b, kind])
                wait_bytes(s2_ref.at[b, kind, pl.ds(0, NLAT - 1)], s3_send.at[b, kind])

    tiles = (11, 6)
    tile0 = (0, 11)

    def bias_home(b, i):
        return RING * (i % 2) + 3 * (i // 2) + b

    def bias_mine(b):
        i = 2 * (z // 3) + ring
        return (lax.rem(z, 3) == b) & (i < tiles[b]), i

    def fold_bias(b):
        total = None
        width = 384 if b == 0 else 256
        if b == 0:
            spread = onehot(iota((C, 384), 1) == key_target(TOK, 256, (C, 1), 0))
        else:
            spread = onehot(iota((96, 256), 1) == key_target(96, 128, (96, 1), 0))
        for c in range(WLON):
            if b == 0:
                got = [ds1_ref[t, pl.ds(QPOS[c], 72, stride=16), :].astype(BF) for t in range(2)]
                part = nn(got[0], spread[0:128]) + nn(got[1][:, 0:64], spread[128:C])
            else:
                part = nn(ds2_ref[pl.ds(QPOS[c], 72, stride=16), :].astype(BF)[:, 0:96], spread)
            if c:
                part = pltpu.roll(part, width - c, 1)
            total = part if total is None else total + part
        total = jnp.concatenate([total, jnp.zeros((8, width), F32)], axis=0)
        lanes = width // 128 - 1
        extra = TAB - 256 if b == 0 else 138 - 128
        for rt in range(5):
            for lt in range(lanes):
                tile = total[16 * rt:16 * rt + 16, 128 * lt:128 * lt + 128]
                bs_ref[tile0[b] + rt * lanes + lt] = tile.astype(BF)
        packed = None
        for rt in range(5):
            tile = total[16 * rt:16 * rt + 16, 128 * lanes:]
            if rt:
                tile = pltpu.roll(tile, extra * rt, 1)
                packed = jnp.where(iota((16, 128), 1) >= extra * rt, tile, packed)
            else:
                packed = tile
        bs_ref[tile0[b] + 5 * lanes] = packed.astype(BF)

    def b_copy(b, i):
        return pltpu.make_async_remote_copy(
            src_ref=bs_ref.at[tile0[b] + i],
            dst_ref=br_ref.at[lon],
            send_sem=b_send.at[tile0[b] + i],
            recv_sem=b_recv,
            device_id={"lon": bias_home(b, i)},
            device_id_type=MESH,
        )

    def bias_send(b):
        for i in range(tiles[b]):
            @pl.when(lon != bias_home(b, i))
            def _():
                b_copy(b, i).start()

            @pl.when(lon == bias_home(b, i))
            def _():
                br_ref[lon] = bs_ref[tile0[b] + i]

    def bias_reduce(b):
        mine, i = bias_mine(b)
        at = tile0[b] + i

        @pl.when(mine)
        def _():
            wait_bytes(br_ref.at[pl.ds(0, NLON - 1)], b_recv)
            acc = br_ref[0].astype(F32)
            for j in range(1, NLON):
                acc = acc + br_ref[j].astype(F32)
            ball_ref[at] = acc.astype(BF)

            def send(k, carry):
                pltpu.make_async_remote_copy(
                    src_ref=ball_ref.at[at],
                    dst_ref=ball_ref.at[at],
                    send_sem=bg_send,
                    recv_sem=bg_recv.at[b],
                    device_id={"lon": at_lon(k)},
                    device_id_type=MESH,
                ).start()
                return carry

            lax.fori_loop(1, NLON, send, 0)

    def bias_finish(b):
        mine, _ = bias_mine(b)

        @pl.when(mine)
        def _():
            wait_bytes(ball_ref.at[pl.ds(tile0[b], tiles[b] - 1)], bg_recv.at[b])

        @pl.when(jnp.logical_not(mine))
        def _():
            wait_bytes(ball_ref.at[pl.ds(tile0[b], tiles[b])], bg_recv.at[b])

        lanes = 2 if b == 0 else 1
        extra = TAB - 256 if b == 0 else 138 - 128
        packed = ball_ref[tile0[b] + 5 * lanes].astype(F32)
        for rt in range(5):
            rows = [ball_ref[tile0[b] + rt * lanes + lt].astype(F32) for lt in range(lanes)]
            rows.append(pltpu.roll(packed, 128 - extra * rt, 1) if rt else packed)
            for i in range(16 if rt < 4 else 8):
                at = 16 * rt + i
                if b == 0:
                    h, a = at // ZONES, at % ZONES
                    for lt in range(3):
                        width = min(128, TAB - 128 * lt)
                        lane = TAB * a + 128 * lt
                        obias_ref[0, h, :, lane:lane + width] = rows[lt][i:i + 1, 0:width]
                else:
                    level, h, a = at // 36, at % 36 // 6, at // 36 * 6 + at % 6
                    for lt in range(2):
                        width = min(128, 138 - 128 * lt)
                        lane = TAB * a + 138 * level + 128 * lt
                        obias_ref[1, h, :, lane:lane + width] = rows[lt][i:i + 1, 0:width]

    def bias_sent(b):
        for i in range(tiles[b]):
            @pl.when(lon != bias_home(b, i))
            def _():
                b_copy(b, i).wait_send()

        @pl.when(bias_mine(b)[0])
        def _():
            wait_bytes(br_ref.at[pl.ds(0, NLON - 1)], bg_send)

    expand_bias(0)
    u1 = load_window(x_ref)
    for load in loads[:4]:
        load.wait()
    out1 = forward(0, u1)
    pl.semaphore_wait(barrier, NLAT - 1 + NLON - 1 + CHIPS - 1 + 2)
    exchange_start(1, out1)
    loads[4].wait()
    ct = load_window(ct_ref)
    exchange_start(0, ct)
    expand_bias(1)
    for s in range(4):
        perm_ref[192 * s:192 * s + 192, :] = onehot(iota((192, HID), 1) == 4 * iota((192, HID), 0) + s)
    row = iota((8 * RING, 1), 0)
    pos = row & 7
    sel_ref[...] = onehot(iota((8 * RING, C // 2), 1) == jnp.where(pos < SHARD, (row >> 3) * SHARD + pos, -1))
    obias_ref[1] = jnp.zeros((HEADS, 1, ZONES * TAB), F32)
    u2 = exchange_finish(1, out1)
    out2 = forward(1, u2)
    exchange_start(2, out2)
    g2 = exchange_finish(0, ct)
    ghid2 = backward_mlp(1, g2)
    attention_grads(1)
    gsec = input_grad(1, ghid2)
    exchange_start(3, gsec)
    grads_mlp(1)
    stage0_send(1, 0)
    stage0_send(1, 1)
    grads_attention(1)
    stage0_send(1, 2)
    fold_bias(1)
    bias_send(1)
    stage1_send(1, 0)
    stage1_send(1, 1)
    store_window(res_ref, exchange_finish(2, out2))
    g1 = exchange_finish(3, gsec)
    ghid1 = backward_mlp(0, g1)
    grads_mlp(0)
    stage0_send(0, 0)
    stage0_send(0, 1)
    attention_grads(0)
    fold_bias(0)
    bias_send(0)
    grads_attention(0)
    stage0_send(0, 2)
    stage1_send(0, 0)
    stage1_reduce(1, 0)
    stage1_reduce(1, 1)
    stage1_send(0, 1)
    bias_reduce(1)
    store_window(gin_ref, input_grad(0, ghid1))
    stage1_reduce(0, 0)
    stage1_reduce(0, 1)
    bias_reduce(0)
    stage2_reduce(1, 0)
    stage2_reduce(1, 1)
    bias_finish(1)
    stage2_reduce(0, 0)
    stage2_reduce(0, 1)
    stage3_finish(1, 0)
    stage3_finish(1, 1)
    bias_finish(0)
    stage3_finish(0, 0)
    stage3_finish(0, 1)
    for b in range(2):
        stages_sent(b)
        bias_sent(b)


def on_device(inputs, cotangent, w_qkv, w_proj, w_up, w_down, earth_bias):
    vm = pl.BlockSpec(memory_space=pltpu.VMEM)
    hbm = pl.BlockSpec(memory_space=pltpu.HBM)
    shapes = (
        jax.ShapeDtypeStruct((6, WLON, 2, C), BF),
        jax.ShapeDtypeStruct((6, WLON, 2, C), BF),
        jax.ShapeDtypeStruct((SHARD, 2, 576), F32),
        jax.ShapeDtypeStruct((SHARD, 2, 192), F32),
        jax.ShapeDtypeStruct((SHARD, 2, 768), F32),
        jax.ShapeDtypeStruct((2, 24, 192), F32),
        jax.ShapeDtypeStruct((2, HEADS, 1, 3312), F32),
    )
    outs = pl.pallas_call(
        kernel,
        out_shape=shapes,
        in_specs=[vm, hbm, hbm, hbm, hbm, hbm, vm],
        out_specs=(vm,) * 7,
        scratch_shapes=[
            pltpu.VMEM((6, WLON, 2, C), BF),
            pltpu.VMEM((2, C, 576), BF),
            pltpu.VMEM((2, C, C), BF),
            pltpu.VMEM((2, C, HID), BF),
            pltpu.VMEM((2, C, HID), BF),
            pltpu.SemaphoreType.DMA((5,)),
            pltpu.VMEM((TOK, C), F32),
            pltpu.VMEM((2, TOK, C), BF),
            pltpu.VMEM((2, TOK, C), F32),
            pltpu.VMEM((2, TOK, 1), F32),
            pltpu.VMEM((2, TOK, 576), BF),
            pltpu.VMEM((HEADS, TOK, TOK), BF),
            pltpu.VMEM((HEADS, TOK, 96), BF),
            pltpu.VMEM((2, TOK, C), BF),
            pltpu.VMEM((2, TOK, C), F32),
            pltpu.VMEM((2, TOK, 1), F32),
            pltpu.VMEM((2, TOK, C), BF),
            pltpu.VMEM((2, TOK, HID), BF),
            pltpu.VMEM((2, TOK, HID), BF),
            pltpu.VMEM((2, TOK, HID), BF),
            pltpu.VMEM((2, TOK, 576), BF),
            pltpu.VMEM((2, TOK, C), BF),
            pltpu.VMEM((2, TOK, C), BF),
            pltpu.VMEM((3, 72, 128), F32),
            pltpu.VMEM((2, 1152, 128), F32),
            pltpu.VMEM((1152, 128), F32),
            pltpu.VMEM((2, 1152, 128), F32),
            pltpu.VMEM((1152, 128), F32),
            pltpu.VMEM((HID, HID), BF),
            pltpu.VMEM((8 * RING, C // 2), BF),
            pltpu.VMEM((4, 3, 48, C), BF),
            pltpu.VMEM((4, 3, 48, C), BF),
            pltpu.VMEM((2, 3, 6, C, 128), BF),
            pltpu.VMEM((2, 3, 3, C, 128), BF),
            pltpu.VMEM((2, 3, 2, 2, C // 2, 128), BF),
            pltpu.VMEM((2, 3, 2, 1, C // 2, 128), BF),
            pltpu.VMEM((2, 2 * CHIPS, 2, C // 2, 128), BF),
            pltpu.VMEM((2, 2 * CHIPS, 1, C // 2, 128), BF),
            pltpu.VMEM((2, 2, RING, 16, 128), BF),
            pltpu.VMEM((2, 2, RING, 16, 128), BF),
            pltpu.VMEM((2, 2, 16, 128), BF),
            pltpu.VMEM((2, 2, 6, 16, 128), BF),
            pltpu.VMEM((17, 16, 128), BF),
            pltpu.VMEM((NLON, 16, 128), BF),
            pltpu.VMEM((17, 16, 128), BF),
            pltpu.SemaphoreType.DMA((4, 3)),
            pltpu.SemaphoreType.DMA((4, 3)),
            pltpu.SemaphoreType.DMA((2, 3)),
            pltpu.SemaphoreType.DMA((2, 3)),
            pltpu.SemaphoreType.DMA((2, 2, 3, 2)),
            pltpu.SemaphoreType.DMA((2, 2)),
            pltpu.SemaphoreType.DMA((2, 2)),
            pltpu.SemaphoreType.DMA((2, 2)),
            pltpu.SemaphoreType.DMA((2, 2)),
            pltpu.SemaphoreType.DMA((2, 2)),
            pltpu.SemaphoreType.DMA((17,)),
            pltpu.SemaphoreType.DMA,
            pltpu.SemaphoreType.DMA,
            pltpu.SemaphoreType.DMA((2,)),
        ],
        compiler_params=pltpu.CompilerParams(
            collective_id=0, has_side_effects=True, vmem_limit_bytes=64 * 1024 * 1024
        ),
        name="earth_blocks",
    )(
        inputs.transpose(1, 2, 0, 3),
        cotangent.transpose(1, 2, 0, 3),
        w_qkv,
        w_proj,
        w_up,
        w_down.transpose(0, 2, 1),
        earth_bias.reshape(2, HEADS, 3312),
    )
    result, grad_inputs, g_qkv, g_proj, g_up, g_down, g_bias = outs
    return (
        result.transpose(2, 0, 1, 3),
        grad_inputs.transpose(2, 0, 1, 3),
        g_qkv.transpose(1, 0, 2),
        g_proj.transpose(1, 0, 2),
        g_up.transpose(1, 0, 2),
        g_down,
        g_bias.reshape(2, 1, 1, HEADS, 3312),
    )


def solution(mesh):
    field = P(None, "lat", "lon", None)
    shard = P(None, "lon", None)
    bias = P(None, "lat", None, None, None)
    return jax.shard_map(
        on_device,
        mesh=mesh,
        in_specs=(field, field, P(), P(), P(), P(), bias),
        out_specs=(field, field, shard, shard, shard, shard, bias),
        check_vma=False,
    )
```

```python
import jax
import jax.numpy as jnp
from jax import lax
from jax.experimental import pallas as pl
from jax.experimental.pallas import tpu as pltpu
from jax.sharding import PartitionSpec as P

BF = jnp.bfloat16
F32 = jnp.float32
MESH = pl.DeviceIdType.MESH

HEADS = 6
C = 192
HID = 768
WLON = 12
ZONES = 12
REACH = 23
TAB = ZONES * REACH
NLAT = 16
NLON = 32
RING = 16
CHIPS = 8
SHARD = 6
TOK = 192
NEG_FILL = -1e30
LN_EPS = 1e-05
SCALE = 32.0 ** -0.5
NORM = 73728.0 ** -0.5

QPOS = [c if c < 6 else c + 2 for c in range(WLON)]
PAD_POS = [6, 7, 14, 15]


def nn(a, b):
    return lax.dot_general(a, b, (((1,), (0,)), ((), ())), preferred_element_type=F32)


def nt(a, b):
    return lax.dot_general(a, b, (((1,), (1,)), ((), ())), preferred_element_type=F32)


def iota(shape, dim):
    return lax.broadcasted_iota(jnp.int32, shape, dim)


def onehot(cond):
    return jnp.where(cond, 1.0, 0.0).astype(BF)


def ln(x):
    mean = jnp.mean(x, axis=-1, keepdims=True)
    centred = x - mean
    inv = lax.rsqrt(jnp.mean(centred * centred, axis=-1, keepdims=True) + LN_EPS)
    return centred * inv, inv


def ln_back(scaled, inv, grad):
    mean_grad = jnp.mean(grad, axis=-1, keepdims=True)
    mean_proj = jnp.mean(grad * scaled, axis=-1, keepdims=True)
    return inv * (grad - mean_grad - scaled * mean_proj)


def gelu_pair(v):
    gauss = jnp.exp(-0.5 * v * v)
    t = 1.0 / (1.0 + (0.3275911 * 0.7071067811865476) * jnp.abs(v))
    poly = t * (
        0.127414796 + t * (-0.142248368 + t * (0.7107068705 + t * (-0.7265760135 + t * 0.5307027145)))
    )
    tail = poly * gauss
    phi = jnp.where(v < 0.0, tail, 1.0 - tail)
    return v * phi, phi + v * gauss * 0.3989422804014327


def key_target(lanes, width, shape, dim):
    y = iota(shape, dim)
    pos = y & 15
    col = jnp.where(pos < 8, pos, pos - 2)
    valid = ((pos & 7) < 6) & (y < lanes)
    return jnp.where(valid, (y >> 4) * REACH + col + (WLON - 1), -1)


def kernel(
    x_ref, ct_hbm, wqkv_hbm, wproj_hbm, wup_hbm, wdown_hbm, eb_ref,
    res_ref, gin_ref, oqkv_ref, oproj_ref, oup_ref, odown_ref, obias_ref,
    ct_ref, wqkv_ref, wproj_ref, wup_ref, wdown_ref, in_sem, win_ref, n1_ref, sc1_ref, inv1_ref, qkv_ref, p1_ref, p2_ref, mix_ref, sc2_ref, inv2_ref, n2_ref,
    act_ref, slope_ref, gpre_ref, gqkv_ref, ghb_ref, g_ref,
    t_ref, bias1_ref, bias2_ref, ds1_ref, ds2_ref,
    perm_ref, sel_ref,
    xs_ref, xr_ref,
    strip_ref, r0_ref, a_du_ref, a_qp_ref, r1_du_ref, r1_qp_ref, s2_ref, r2_ref, s3_ref, r3_ref,
    bs_ref, br_ref, ball_ref,
    x_send, x_recv, s0_send, s0_recv, s1_send, s1_recv, s2_send, s2_recv, s3_send, s3_recv,
    b_send, b_recv, bg_send, bg_recv,
):
    lat = lax.axis_index("lat")
    lon = lax.axis_index("lon")

    def at_lat(k):
        return lax.rem(lat + k + NLAT, NLAT)

    def at_lon(k):
        return lax.rem(lon + k + NLON, NLON)

    loads = [
        pltpu.make_async_copy(src, dst, in_sem.at[i])
        for i, (src, dst) in enumerate(
            (
                (wqkv_hbm, wqkv_ref),
                (wproj_hbm, wproj_ref),
                (wup_hbm, wup_ref),
                (wdown_hbm, wdown_ref),
                (ct_hbm, ct_ref),
            )
        )
    ]
    for load in loads:
        load.start()

    barrier = pltpu.get_barrier_semaphore()

    def greet_lat(k, carry):
        pl.semaphore_signal(barrier, inc=1, device_id={"lat": at_lat(k)}, device_id_type=MESH)
        return carry

    def greet_lon(k, carry):
        pl.semaphore_signal(barrier, inc=1, device_id={"lon": at_lon(k)}, device_id_type=MESH)
        return carry

    lax.fori_loop(1, NLAT, greet_lat, 0)
    lax.fori_loop(1, NLON, greet_lon, 0)
    def greet_far(k, carry):
        to = {"lat": lax.rem(lat + 2 * k, NLAT), "lon": lax.rem(lon + RING, NLON)}
        pl.semaphore_signal(barrier, inc=1, device_id=to, device_id_type=MESH)
        return carry

    lax.fori_loop(1, CHIPS, greet_far, 0)
    for k in (-1, 1):
        pl.semaphore_signal(
            barrier, inc=1, device_id={"lat": at_lat(k), "lon": at_lon(k)}, device_id_type=MESH
        )

    lane = iota((1, C), 1) >> 5
    hm = [onehot(lane == h) for h in range(HEADS)]
    eye = onehot(iota((C, C), 0) == iota((C, C), 1))
    tgt1 = key_target(TOK, 256, (1, 256), 1)
    tgt2 = key_target(96, 128, (1, 128), 1)

    def load_window(src):
        win_ref[...] = jnp.zeros((TOK, C), F32)
        for r in range(6):
            for c in range(WLON):
                v = src[r, c].astype(F32)
                for lev in range(2):
                    at = 96 * lev + 16 * r + QPOS[c]
                    win_ref[at:at + 1, :] = v[lev:lev + 1]
        return win_ref[...]

    def store_window(dst, val):
        for r in range(6):
            for c in range(WLON):
                at = 16 * r + QPOS[c]
                dst[r, c] = jnp.concatenate([val[at:at + 1], val[at + 96:at + 97]], axis=0).astype(BF)

    def group(val, lev, row, half):
        at = 96 * lev + 16 * row + 8 * half
        return val[at:at + 8]

    def strip(val, row0, half):
        return jnp.concatenate(
            [group(val, lev, row0 + r, half) for lev in range(2) for r in range(3)], axis=0
        ).astype(BF)

    def exchange_copies(idx):
        step = -1 if idx < 2 else 1
        targets = (
            {"lon": at_lon(step)},
            {"lat": at_lat(step)},
            {"lat": at_lat(step), "lon": at_lon(step)},
        )
        return [
            pltpu.make_async_remote_copy(
                src_ref=xs_ref.at[idx, i],
                dst_ref=xr_ref.at[idx, i],
                send_sem=x_send.at[idx, i],
                recv_sem=x_recv.at[idx, i],
                device_id=targets[i],
                device_id_type=MESH,
            )
            for i in range(3)
        ]

    def exchange_start(idx, val):
        if idx < 2:
            parts = (strip(val, 3, 0), strip(val, 0, 1), strip(val, 0, 0))
        else:
            parts = (strip(val, 0, 1), strip(val, 3, 0), strip(val, 3, 1))
        for i, copy in enumerate(exchange_copies(idx)):
            xs_ref[idx, i] = parts[i]
            copy.start()

    def exchange_finish(idx, val):
        for copy in exchange_copies(idx):
            copy.wait()
        got = [xr_ref[idx, i].astype(F32) for i in range(3)]
        row_near = 0 if idx < 2 else 3
        half_near = 0 if idx < 2 else 1
        rows = []
        for lev in range(2):
            old = 1 - lev
            for row in range(6):
                near_row = (row < 3) == (row_near == 0)
                r = row % 3
                pieces = []
                for half in range(2):
                    near_half = half == half_near
                    at = 24 * old + 8 * r
                    if near_row and near_half:
                        piece = group(val, old, (3 if idx < 2 else 0) + r, 1 - half)
                    elif near_row:
                        piece = got[0][at:at + 8]
                    elif near_half:
                        piece = got[1][at:at + 8]
                    else:
                        piece = got[2][at:at + 8]
                    pieces.append(piece)
                rows += pieces
        return jnp.concatenate(rows, axis=0)

    def load_table(b):
        t_ref[...] = jnp.zeros_like(t_ref)
        for a in range(ZONES):
            if b == 0:
                rows = pl.ds(a, HEADS, stride=ZONES)
            else:
                rows = pl.ds(36 * (a // 6) + a % 6, HEADS, stride=6)
            for lt in range(3):
                width = min(128, TAB - 128 * lt)
                lane = TAB * a + 128 * lt
                piece = eb_ref[b, :, lane:lane + width]
                if width < 128:
                    piece = jnp.concatenate([piece, jnp.zeros((HEADS, 128 - width), F32)], axis=1)
                t_ref[lt, rows, :] = piece
        return jnp.concatenate([t_ref[lt] for lt in range(3)], axis=1)

    def split3(v):
        hi = v.astype(BF)
        rest = v - hi.astype(F32)
        mid = rest.astype(BF)
        return hi, mid, (rest - mid.astype(F32)).astype(BF)

    def expand_bias(b):
        table = load_table(b)
        if b == 0:
            spread = onehot(iota((384, 256), 0) == tgt1)
            mask = jnp.broadcast_to(jnp.where(tgt1 < 0, NEG_FILL, 0.0), (72, 256))
        else:
            spread = jnp.concatenate(
                [onehot(iota((384, 128), 0) == jnp.where(tgt2 < 0, -1, tgt2 + 138 * lv)) for lv in range(2)], axis=1
            )
            row = iota((72, 1), 0)
            row = jnp.where(row >= 36, row - 36, row)
            far_row = jnp.where(lax.rem(row, 6) >= 3, 1, 0)
            far_key = jnp.where(iota((1, 128), 1) >= 48, 1, 0)
            last = jnp.where(lat == NLAT - 1, 1, 0)
            cut = (far_row + far_key) * last == 1
            mask = jnp.where(cut | (tgt2 < 0), NEG_FILL, 0.0)
            low = iota((72, 1), 0) < 36
        for c in range(WLON):
            rolled = pltpu.roll(table, c, 1) if c else table
            full = sum(nn(p, spread) for p in split3(rolled))
            if b == 0:
                full = full + mask
                for t in range(2):
                    bias1_ref[t, pl.ds(QPOS[c], 72, stride=16), :] = full[:, 128 * t:128 * t + 128]
            else:
                bias2_ref[pl.ds(QPOS[c], 72, stride=16), :] = jnp.where(low, full[:, 0:128], full[:, 128:256]) + mask
        for p in PAD_POS:
            if b == 0:
                for t in range(2):
                    bias1_ref[t, pl.ds(p, 72, stride=16), :] = mask[:, 128 * t:128 * t + 128]
            else:
                bias2_ref[pl.ds(p, 72, stride=16), :] = mask

    def head_bias(b, h, seg):
        if b == 0:
            rows = slice(TOK * h, TOK * h + TOK)
            return jnp.concatenate([bias1_ref[0, rows, :], bias1_ref[1, rows, 0:64]], axis=1)
        at = 96 * (HEADS * seg + h)
        return bias2_ref[at:at + 96, 0:96]

    segments = ((0, TOK),), ((0, 96), (96, 96))

    def forward(b, u):
        sc1, inv1 = ln(u)
        n1 = sc1.astype(BF)
        n1_ref[b] = n1
        sc1_ref[b] = sc1
        inv1_ref[b] = inv1
        qkv_ref[b] = nn(n1, wqkv_ref[b]).astype(BF)
        q = qkv_ref[b, :, 0:C]
        k = qkv_ref[b, :, C:2 * C]
        v = qkv_ref[b, :, 2 * C:3 * C]
        cases = [(seg, slice(start, start + size), h) for seg, (start, size) in enumerate(segments[b]) for h in range(HEADS)]
        qh = [q * hm[h] for h in range(HEADS)]
        vh = [v * hm[h] for h in range(HEADS)]
        scores = [nt(qh[h][rows], k[rows]) for _, rows, h in cases]
        probs = []
        for (seg, rows, h), raw in zip(cases, scores):
            full = raw * SCALE + head_bias(b, h, seg)
            e = jnp.exp(full - jnp.max(full, axis=-1, keepdims=True))
            p = (e * (1.0 / jnp.sum(e, axis=-1, keepdims=True))).astype(BF)
            if b == 0:
                p1_ref[h] = p
            else:
                p2_ref[h, rows, :] = p
            probs.append(p)
        mixed = [None] * len(segments[b])
        for (seg, rows, h), p in zip(cases, probs):
            part = nn(p, vh[h][rows])
            mixed[seg] = part if h == 0 else mixed[seg] + part
        for seg, (start, size) in enumerate(segments[b]):
            mix_ref[b, start:start + size, :] = mixed[seg].astype(BF)
        hidden = (u + nn(mix_ref[b], wproj_ref[b])).astype(BF).astype(F32)
        sc2, inv2 = ln(hidden)
        n2 = sc2.astype(BF)
        sc2_ref[b] = sc2
        inv2_ref[b] = inv2
        n2_ref[b] = n2
        acc = hidden
        for c in range(0, HID, 256):
            act, slope = gelu_pair(nn(n2, wup_ref[b, :, c:c + 256]))
            act = act.astype(BF)
            act_ref[b, :, c:c + 256] = act
            slope_ref[b, :, c:c + 256] = slope.astype(BF)
            acc = acc + nt(act, wdown_ref[b, :, c:c + 256])
        return acc.astype(BF).astype(F32)

    def backward_mlp(b, gf):
        g = gf.astype(BF)
        g_ref[b] = g
        gn2 = jnp.zeros((TOK, C), F32)
        for c in range(0, HID, 256):
            gact = nn(g, wdown_ref[b, :, c:c + 256])
            gpre = (gact * slope_ref[b, :, c:c + 256].astype(F32)).astype(BF)
            gpre_ref[b, :, c:c + 256] = gpre
            gn2 = gn2 + nt(gpre, wup_ref[b, :, c:c + 256])
        ghid = gf + ln_back(sc2_ref[b], inv2_ref[b], gn2)
        ghb_ref[b] = ghid.astype(BF)
        return ghid

    def attention_start(b):
        gmix = nt(ghb_ref[b], wproj_ref[b]).astype(BF)
        q = qkv_ref[b, :, 0:C]
        v = qkv_ref[b, :, 2 * C:3 * C]
        cases = [(seg, slice(start, start + size), h) for seg, (start, size) in enumerate(segments[b]) for h in range(HEADS)]
        gh = [gmix * hm[h] for h in range(HEADS)]
        gps = [nt(gh[h][rows], v[rows]) for _, rows, h in cases]
        spans = [slice(start, start + size) for start, size in segments[b]]
        qt = [nt(eye, q[rows]).astype(BF) for rows in spans]
        gmt = [nt(eye, gmix[rows]).astype(BF) for rows in spans]
        return cases, gps, qt, gmt

    def attention_grads(b, started):
        cases, gps, qt, gmt = started
        k = qkv_ref[b, :, C:2 * C]
        kh = [k * hm[h] for h in range(HEADS)]
        gvt = []
        dsbs = []
        for (seg, rows, h), gp in zip(cases, gps):
            pb = p1_ref[h] if b == 0 else p2_ref[h, rows, :]
            gvt.append(nn(gmt[seg][32 * h:32 * h + 32], pb))
            pf = pb.astype(F32)
            ds = pf * (gp - jnp.sum(gp * pf, axis=-1, keepdims=True))
            if b == 0:
                ds1_ref[0, TOK * h:TOK * h + TOK, :] = ds[:, 0:128]
                ds1_ref[1, TOK * h:TOK * h + TOK, 0:64] = ds[:, 128:192]
            else:
                at = 96 * (HEADS * seg + h)
                ds2_ref[at:at + 96, 0:96] = ds
            dsbs.append(ds.astype(BF))
        gkt = [nn(qt[seg][32 * h:32 * h + 32], dsb) for (seg, _, h), dsb in zip(cases, dsbs)]
        gq = [None] * len(segments[b])
        for (seg, rows, h), dsb in zip(cases, dsbs):
            part = nn(dsb, kh[h][rows])
            gq[seg] = part if h == 0 else gq[seg] + part
        for seg, (start, size) in enumerate(segments[b]):
            rows = slice(start, start + size)
            heads = slice(HEADS * seg, HEADS * seg + HEADS)
            small = eye if size == C else eye[0:size, 0:size]
            gk = nt(small, (jnp.concatenate(gkt[heads], axis=0) * SCALE).astype(BF)).astype(BF)
            gv = nt(small, jnp.concatenate(gvt[heads], axis=0).astype(BF)).astype(BF)
            gqkv_ref[b, rows, 0:C] = (gq[seg] * SCALE).astype(BF)
            gqkv_ref[b, rows, C:2 * C] = gk
            gqkv_ref[b, rows, 2 * C:3 * C] = gv

    def input_grad(b, ghid):
        gn1 = nt(gqkv_ref[b], wqkv_ref[b])
        return (ghid + ln_back(sc1_ref[b], inv1_ref[b], gn1)).astype(BF).astype(F32)

    def put_strips(b, t, s, val):
        val = (val * NORM).astype(BF)
        for i in range(val.shape[1] // 128):
            strip_ref[b, t, s + i] = val[:, 128 * i:128 * i + 128]

    def grads_mlp(b):
        actt = nt(perm_ref[...], act_ref[b]).astype(BF)
        g = g_ref[b]
        for pair in range(2):
            at = 384 * pair
            both = [nn(actt[at + 192 * i:at + 192 * i + 192], g) for i in range(2)]
            put_strips(b, 0, 3 * pair, jnp.concatenate(both, axis=1))
        n2t = nt(eye, n2_ref[b]).astype(BF)
        for s in range(3):
            put_strips(b, 1, 2 * s, nn(n2t, gpre_ref[b, :, 256 * s:256 * s + 256]))

    def grads_attention(b):
        n1t = nt(eye, n1_ref[b]).astype(BF)
        mixt = nt(eye, mix_ref[b]).astype(BF)
        put_strips(b, 2, 0, nn(n1t, gqkv_ref[b, :, 0:256]))
        put_strips(b, 2, 2, nn(n1t, gqkv_ref[b, :, 256:512]))
        rest = [nn(n1t, gqkv_ref[b, :, 512:576]), nn(mixt, ghb_ref[b])]
        put_strips(b, 2, 4, jnp.concatenate(rest, axis=1))

    core = lax.rem(lat, 2)
    chip = lat // 2
    ring = lon // RING
    z = lax.rem(lon, RING)
    half = C // 2
    a_refs = (a_du_ref, a_qp_ref)

    def far_first(i):
        step = (i + 1) // 2
        return lax.rem(z + RING // 2 + step * (1 - 2 * lax.rem(i, 2)), RING)

    r1_refs = (r1_du_ref, r1_qp_ref)

    def place(b):
        return chip if b else lax.rem(chip + 4, 8)

    def owned(b, kind):
        at = place(b)
        if kind == 0:
            return at // 3 == core, at - 3 * core
        return (at >= 6) | (at == 3 - 3 * core), jnp.where(at >= 6, at - 6, 2)

    def owner(b, kind, i):
        if kind == 0:
            at = 3 * core + i
        else:
            at = 6 + i if i < 2 else 3 - 3 * core
        at = at if b else lax.rem(at + 4, 8)
        return 2 * at + core

    def wait_bytes(ref, sem):
        pltpu.make_async_copy(ref, ref, sem).wait()

    def s0_copy(b, t):
        return pltpu.make_async_remote_copy(
            src_ref=strip_ref.at[b, t, pl.ds(3 - 3 * core, 3)],
            dst_ref=r0_ref.at[b, t],
            send_sem=s0_send.at[b, t],
            recv_sem=s0_recv.at[b, t],
            device_id={"lat": lat + 1 - 2 * core},
            device_id_type=MESH,
        )

    def stage0_send(b, t):
        s0_copy(b, t).start()

    def s1_copy(b, kind, i, g):
        return pltpu.make_async_remote_copy(
            src_ref=a_refs[kind].at[b, i, g],
            dst_ref=r1_refs[kind].at[b, CHIPS * ring + chip],
            send_sem=s1_send.at[b, kind, i, g],
            recv_sem=s1_recv.at[b, kind],
            device_id={"lat": owner(b, kind, i), "lon": RING * g + z},
            device_id_type=MESH,
        )

    def s1_here(b, kind, i, g):
        return (lat == owner(b, kind, i)) & (ring == g)

    def stage1_send(b, kind):
        groups = (0, 1) if kind == 0 else (2,)
        for t in groups:
            s0_copy(b, t).wait_recv()
        for i in range(3):
            for part, t in enumerate(groups):
                both = strip_ref[b, t, 3 * core + i].astype(F32) + r0_ref[b, t, i].astype(F32)
                for g in range(2):
                    a_refs[kind][b, i, g, part] = both[half * g:half * g + half].astype(BF)
            for g in range(2):
                here = s1_here(b, kind, i, g)

                @pl.when(jnp.logical_not(here))
                def _():
                    s1_copy(b, kind, i, g).start()

                @pl.when(here)
                def _():
                    r1_refs[kind][b, CHIPS * ring + chip] = a_refs[kind][b, i, g]

    def stage1_reduce(b, kind):
        mine, _ = owned(b, kind)
        parts = 2 if kind == 0 else 1

        @pl.when(mine)
        def _():
            ref = r1_refs[kind]
            wait_bytes(ref.at[b, pl.ds(0, 2 * CHIPS - 1)], s1_recv.at[b, kind])
            spread = []
            for part in range(parts):
                acc = ref[b, 0, part].astype(F32)
                for i in range(1, 2 * CHIPS):
                    acc = acc + ref[b, i, part].astype(F32)
                spread.append(nn(sel_ref[...], acc.astype(BF)))
            if parts == 1:
                spread.append(jnp.zeros((8 * RING, 128), F32))
            for j in range(RING):
                tile = jnp.concatenate([v[8 * j:8 * j + 8] for v in spread], axis=0)
                s2_ref[b, kind, j] = tile.astype(BF)
            r2_ref[b, kind, z] = s2_ref[b, kind, z]

            def send(i, carry):
                to = far_first(i)
                pltpu.make_async_remote_copy(
                    src_ref=s2_ref.at[b, kind, to],
                    dst_ref=r2_ref.at[b, kind, z],
                    send_sem=s2_send.at[b, kind],
                    recv_sem=s2_recv.at[b, kind],
                    device_id={"lon": RING * ring + to},
                    device_id_type=MESH,
                ).start()
                return carry

            lax.fori_loop(0, RING - 1, send, 0)

    def stage2_reduce(b, kind):
        mine, i = owned(b, kind)
        which = 3 * core + i

        @pl.when(mine)
        def _():
            wait_bytes(r2_ref.at[b, kind, pl.ds(0, RING - 1)], s2_recv.at[b, kind])
            acc = r2_ref[b, kind, 0].astype(F32)
            for j in range(1, RING):
                acc = acc + r2_ref[b, kind, j].astype(F32)
            total = acc.astype(BF)
            s3_ref[b, kind] = total
            r3_ref[b, kind, which] = total

            def send(k, carry):
                pltpu.make_async_remote_copy(
                    src_ref=s3_ref.at[b, kind],
                    dst_ref=r3_ref.at[b, kind, which],
                    send_sem=s3_send.at[b, kind],
                    recv_sem=s3_recv.at[b, kind],
                    device_id={"lat": at_lat(k)},
                    device_id_type=MESH,
                ).start()
                return carry

            lax.fori_loop(1, NLAT, send, 0)

    def put_rows(ref, b, val):
        for i in range(SHARD):
            ref[i, b:b + 1, :] = val[i:i + 1]

    def stage3_finish(b, kind):
        mine, _ = owned(b, kind)

        @pl.when(mine)
        def _():
            wait_bytes(r3_ref.at[b, kind, pl.ds(0, 5)], s3_recv.at[b, kind])

        @pl.when(jnp.logical_not(mine))
        def _():
            wait_bytes(r3_ref.at[b, kind], s3_recv.at[b, kind])

        tiles = [r3_ref[b, kind, s].astype(F32) for s in range(6)]
        first = jnp.concatenate([v[0:8] for v in tiles], axis=1)
        if kind == 0:
            for s in range(4):
                part = first[:, 192 * s:192 * s + 192]
                for i in range(SHARD):
                    odown_ref[b, 4 * i + s:4 * i + s + 1, :] = part[i:i + 1]
            put_rows(oup_ref, b, jnp.concatenate([v[8:16] for v in tiles], axis=1))
        else:
            put_rows(oqkv_ref, b, first[:, 0:576])
            put_rows(oproj_ref, b, first[:, 576:768])

    def stages_sent(b):
        for t in range(3):
            s0_copy(b, t).wait_send()
        for kind in range(2):
            for i in range(3):
                for g in range(2):
                    @pl.when(jnp.logical_not(s1_here(b, kind, i, g)))
                    def _():
                        s1_copy(b, kind, i, g).wait_send()

            @pl.when(owned(b, kind)[0])
            def _():
                wait_bytes(s2_ref.at[b, kind, pl.ds(0, RING - 1)], s2_send.at[b, kind])
                wait_bytes(s2_ref.at[b, kind, pl.ds(0, NLAT - 1)], s3_send.at[b, kind])

    tiles = (11, 6)
    tile0 = (0, 11)

    def bias_home(b, i):
        return RING * (i % 2) + 3 * (i // 2) + b

    def bias_mine(b):
        i = 2 * (z // 3) + ring
        return (lax.rem(z, 3) == b) & (i < tiles[b]), i

    def fold_bias(b):
        total = None
        width = 384 if b == 0 else 256
        if b == 0:
            spread = onehot(iota((C, 384), 1) == key_target(TOK, 256, (C, 1), 0))
        else:
            spread = onehot(iota((96, 256), 1) == key_target(96, 128, (96, 1), 0))
        for c in range(WLON):
            if b == 0:
                got = [ds1_ref[t, pl.ds(QPOS[c], 72, stride=16), :].astype(BF) for t in range(2)]
                part = nn(got[0], spread[0:128]) + nn(got[1][:, 0:64], spread[128:C])
            else:
                part = nn(ds2_ref[pl.ds(QPOS[c], 72, stride=16), :].astype(BF)[:, 0:96], spread)
            if c:
                part = pltpu.roll(part, width - c, 1)
            total = part if total is None else total + part
        total = jnp.concatenate([total, jnp.zeros((8, width), F32)], axis=0)
        lanes = width // 128 - 1
        extra = TAB - 256 if b == 0 else 138 - 128
        for rt in range(5):
            for lt in range(lanes):
                tile = total[16 * rt:16 * rt + 16, 128 * lt:128 * lt + 128]
                bs_ref[tile0[b] + rt * lanes + lt] = tile.astype(BF)
        packed = None
        for rt in range(5):
            tile = total[16 * rt:16 * rt + 16, 128 * lanes:]
            if rt:
                tile = pltpu.roll(tile, extra * rt, 1)
                packed = jnp.where(iota((16, 128), 1) >= extra * rt, tile, packed)
            else:
                packed = tile
        bs_ref[tile0[b] + 5 * lanes] = packed.astype(BF)

    def b_copy(b, i):
        return pltpu.make_async_remote_copy(
            src_ref=bs_ref.at[tile0[b] + i],
            dst_ref=br_ref.at[lon],
            send_sem=b_send.at[tile0[b] + i],
            recv_sem=b_recv,
            device_id={"lon": bias_home(b, i)},
            device_id_type=MESH,
        )

    def bias_send(b):
        for i in range(tiles[b]):
            @pl.when(lon != bias_home(b, i))
            def _():
                b_copy(b, i).start()

            @pl.when(lon == bias_home(b, i))
            def _():
                br_ref[lon] = bs_ref[tile0[b] + i]

    def bias_reduce(b):
        mine, i = bias_mine(b)
        at = tile0[b] + i

        @pl.when(mine)
        def _():
            wait_bytes(br_ref.at[pl.ds(0, NLON - 1)], b_recv)
            acc = br_ref[0].astype(F32)
            for j in range(1, NLON):
                acc = acc + br_ref[j].astype(F32)
            ball_ref[at] = acc.astype(BF)

            def send_to(to):
                pltpu.make_async_remote_copy(
                    src_ref=ball_ref.at[at],
                    dst_ref=ball_ref.at[at],
                    send_sem=bg_send,
                    recv_sem=bg_recv.at[b],
                    device_id={"lon": to},
                    device_id_type=MESH,
                ).start()

            def send(i, carry):
                to = far_first(i)
                send_to(RING * (1 - ring) + to)
                send_to(RING * ring + to)
                return carry

            lax.fori_loop(0, RING - 1, send, 0)
            send_to(RING * (1 - ring) + z)

    def bias_finish(b):
        mine, _ = bias_mine(b)

        @pl.when(mine)
        def _():
            wait_bytes(ball_ref.at[pl.ds(tile0[b], tiles[b] - 1)], bg_recv.at[b])

        @pl.when(jnp.logical_not(mine))
        def _():
            wait_bytes(ball_ref.at[pl.ds(tile0[b], tiles[b])], bg_recv.at[b])

        lanes = 2 if b == 0 else 1
        extra = TAB - 256 if b == 0 else 138 - 128
        packed = ball_ref[tile0[b] + 5 * lanes].astype(F32)
        for rt in range(5):
            rows = [ball_ref[tile0[b] + rt * lanes + lt].astype(F32) for lt in range(lanes)]
            rows.append(pltpu.roll(packed, 128 - extra * rt, 1) if rt else packed)
            for i in range(16 if rt < 4 else 8):
                at = 16 * rt + i
                if b == 0:
                    h, a = at // ZONES, at % ZONES
                    for lt in range(3):
                        width = min(128, TAB - 128 * lt)
                        lane = TAB * a + 128 * lt
                        obias_ref[0, h, :, lane:lane + width] = rows[lt][i:i + 1, 0:width]
                else:
                    level, h, a = at // 36, at % 36 // 6, at // 36 * 6 + at % 6
                    for lt in range(2):
                        width = min(128, 138 - 128 * lt)
                        lane = TAB * a + 138 * level + 128 * lt
                        obias_ref[1, h, :, lane:lane + width] = rows[lt][i:i + 1, 0:width]

    def bias_sent(b):
        for i in range(tiles[b]):
            @pl.when(lon != bias_home(b, i))
            def _():
                b_copy(b, i).wait_send()

        @pl.when(bias_mine(b)[0])
        def _():
            wait_bytes(br_ref.at[pl.ds(0, NLON - 1)], bg_send)

    expand_bias(0)
    u1 = load_window(x_ref)
    for load in loads[:4]:
        load.wait()
    out1 = forward(0, u1)
    pl.semaphore_wait(barrier, NLAT - 1 + NLON - 1 + CHIPS - 1 + 2)
    exchange_start(1, out1)
    loads[4].wait()
    ct = load_window(ct_ref)
    exchange_start(0, ct)
    expand_bias(1)
    for s in range(4):
        perm_ref[192 * s:192 * s + 192, :] = onehot(iota((192, HID), 1) == 4 * iota((192, HID), 0) + s)
    row = iota((8 * RING, 1), 0)
    pos = row & 7
    sel_ref[...] = onehot(iota((8 * RING, C // 2), 1) == jnp.where(pos < SHARD, (row >> 3) * SHARD + pos, -1))
    obias_ref[1] = jnp.zeros((HEADS, 1, ZONES * TAB), F32)
    u2 = exchange_finish(1, out1)
    out2 = forward(1, u2)
    exchange_start(2, out2)
    g2 = exchange_finish(0, ct)
    ghid2 = backward_mlp(1, g2)
    attention_grads(1, attention_start(1))
    gsec = input_grad(1, ghid2)
    exchange_start(3, gsec)
    grads_mlp(1)
    stage0_send(1, 0)
    stage0_send(1, 1)
    grads_attention(1)
    stage0_send(1, 2)
    fold_bias(1)
    bias_send(1)
    stage1_send(1, 0)
    stage1_send(1, 1)
    store_window(res_ref, exchange_finish(2, out2))
    g1 = exchange_finish(3, gsec)
    ghid1 = backward_mlp(0, g1)
    grads_mlp(0)
    stage0_send(0, 0)
    stage0_send(0, 1)
    started = attention_start(0)
    stage1_send(0, 0)
    attention_grads(0, started)
    grads_attention(0)
    stage0_send(0, 2)
    fold_bias(0)
    bias_send(0)
    stage1_send(0, 1)
    stage1_reduce(1, 0)
    stage1_reduce(1, 1)
    bias_reduce(1)
    store_window(gin_ref, input_grad(0, ghid1))
    stage1_reduce(0, 0)
    stage1_reduce(0, 1)
    bias_reduce(0)
    stage2_reduce(1, 0)
    stage2_reduce(1, 1)
    bias_finish(1)
    stage2_reduce(0, 0)
    stage2_reduce(0, 1)
    stage3_finish(1, 0)
    stage3_finish(1, 1)
    bias_finish(0)
    stage3_finish(0, 0)
    stage3_finish(0, 1)
    for b in range(2):
        stages_sent(b)
        bias_sent(b)


def on_device(inputs, cotangent, w_qkv, w_proj, w_up, w_down, earth_bias):
    vm = pl.BlockSpec(memory_space=pltpu.VMEM)
    hbm = pl.BlockSpec(memory_space=pltpu.HBM)
    shapes = (
        jax.ShapeDtypeStruct((6, WLON, 2, C), BF),
        jax.ShapeDtypeStruct((6, WLON, 2, C), BF),
        jax.ShapeDtypeStruct((SHARD, 2, 576), F32),
        jax.ShapeDtypeStruct((SHARD, 2, 192), F32),
        jax.ShapeDtypeStruct((SHARD, 2, 768), F32),
        jax.ShapeDtypeStruct((2, 24, 192), F32),
        jax.ShapeDtypeStruct((2, HEADS, 1, 3312), F32),
    )
    outs = pl.pallas_call(
        kernel,
        out_shape=shapes,
        in_specs=[vm, hbm, hbm, hbm, hbm, hbm, vm],
        out_specs=(vm,) * 7,
        scratch_shapes=[
            pltpu.VMEM((6, WLON, 2, C), BF),
            pltpu.VMEM((2, C, 576), BF),
            pltpu.VMEM((2, C, C), BF),
            pltpu.VMEM((2, C, HID), BF),
            pltpu.VMEM((2, C, HID), BF),
            pltpu.SemaphoreType.DMA((5,)),
            pltpu.VMEM((TOK, C), F32),
            pltpu.VMEM((2, TOK, C), BF),
            pltpu.VMEM((2, TOK, C), F32),
            pltpu.VMEM((2, TOK, 1), F32),
            pltpu.VMEM((2, TOK, 576), BF),
            pltpu.VMEM((HEADS, TOK, TOK), BF),
            pltpu.VMEM((HEADS, TOK, 96), BF),
            pltpu.VMEM((2, TOK, C), BF),
            pltpu.VMEM((2, TOK, C), F32),
            pltpu.VMEM((2, TOK, 1), F32),
            pltpu.VMEM((2, TOK, C), BF),
            pltpu.VMEM((2, TOK, HID), BF),
            pltpu.VMEM((2, TOK, HID), BF),
            pltpu.VMEM((2, TOK, HID), BF),
            pltpu.VMEM((2, TOK, 576), BF),
            pltpu.VMEM((2, TOK, C), BF),
            pltpu.VMEM((2, TOK, C), BF),
            pltpu.VMEM((3, 72, 128), F32),
            pltpu.VMEM((2, 1152, 128), F32),
            pltpu.VMEM((1152, 128), F32),
            pltpu.VMEM((2, 1152, 128), F32),
            pltpu.VMEM((1152, 128), F32),
            pltpu.VMEM((HID, HID), BF),
            pltpu.VMEM((8 * RING, C // 2), BF),
            pltpu.VMEM((4, 3, 48, C), BF),
            pltpu.VMEM((4, 3, 48, C), BF),
            pltpu.VMEM((2, 3, 6, C, 128), BF),
            pltpu.VMEM((2, 3, 3, C, 128), BF),
            pltpu.VMEM((2, 3, 2, 2, C // 2, 128), BF),
            pltpu.VMEM((2, 3, 2, 1, C // 2, 128), BF),
            pltpu.VMEM((2, 2 * CHIPS, 2, C // 2, 128), BF),
            pltpu.VMEM((2, 2 * CHIPS, 1, C // 2, 128), BF),
            pltpu.VMEM((2, 2, RING, 16, 128), BF),
            pltpu.VMEM((2, 2, RING, 16, 128), BF),
            pltpu.VMEM((2, 2, 16, 128), BF),
            pltpu.VMEM((2, 2, 6, 16, 128), BF),
            pltpu.VMEM((17, 16, 128), BF),
            pltpu.VMEM((NLON, 16, 128), BF),
            pltpu.VMEM((17, 16, 128), BF),
            pltpu.SemaphoreType.DMA((4, 3)),
            pltpu.SemaphoreType.DMA((4, 3)),
            pltpu.SemaphoreType.DMA((2, 3)),
            pltpu.SemaphoreType.DMA((2, 3)),
            pltpu.SemaphoreType.DMA((2, 2, 3, 2)),
            pltpu.SemaphoreType.DMA((2, 2)),
            pltpu.SemaphoreType.DMA((2, 2)),
            pltpu.SemaphoreType.DMA((2, 2)),
            pltpu.SemaphoreType.DMA((2, 2)),
            pltpu.SemaphoreType.DMA((2, 2)),
            pltpu.SemaphoreType.DMA((17,)),
            pltpu.SemaphoreType.DMA,
            pltpu.SemaphoreType.DMA,
            pltpu.SemaphoreType.DMA((2,)),
        ],
        compiler_params=pltpu.CompilerParams(
            collective_id=0, has_side_effects=True, vmem_limit_bytes=64 * 1024 * 1024
        ),
        name="earth_blocks",
    )(
        inputs.transpose(1, 2, 0, 3),
        cotangent.transpose(1, 2, 0, 3),
        w_qkv,
        w_proj,
        w_up,
        w_down.transpose(0, 2, 1),
        earth_bias.reshape(2, HEADS, 3312),
    )
    result, grad_inputs, g_qkv, g_proj, g_up, g_down, g_bias = outs
    return (
        result.transpose(2, 0, 1, 3),
        grad_inputs.transpose(2, 0, 1, 3),
        g_qkv.transpose(1, 0, 2),
        g_proj.transpose(1, 0, 2),
        g_up.transpose(1, 0, 2),
        g_down,
        g_bias.reshape(2, 1, 1, HEADS, 3312),
    )


def solution(mesh):
    field = P(None, "lat", "lon", None)
    shard = P(None, "lon", None)
    bias = P(None, "lat", None, None, None)
    return jax.shard_map(
        on_device,
        mesh=mesh,
        in_specs=(field, field, P(), P(), P(), P(), bias),
        out_specs=(field, field, shard, shard, shard, shard, bias),
        check_vma=False,
    )
```

```python
import jax
import jax.numpy as jnp
from jax import lax
from jax.experimental import pallas as pl
from jax.experimental.pallas import tpu as pltpu
from jax.sharding import PartitionSpec as P

BF = jnp.bfloat16
F32 = jnp.float32
MESH = pl.DeviceIdType.MESH

HEADS = 6
C = 192
HID = 768
WLON = 12
ZONES = 12
REACH = 23
TAB = ZONES * REACH
NLAT = 16
NLON = 32
RING = 16
CHIPS = 8
SHARD = 6
TOK = 192
NEG_FILL = -1e30
LN_EPS = 1e-05
SCALE = 32.0 ** -0.5
NORM = 73728.0 ** -0.5

QPOS = [c if c < 6 else c + 2 for c in range(WLON)]
PAD_POS = [6, 7, 14, 15]


def nn(a, b):
    return lax.dot_general(a, b, (((1,), (0,)), ((), ())), preferred_element_type=F32)


def nt(a, b):
    return lax.dot_general(a, b, (((1,), (1,)), ((), ())), preferred_element_type=F32)


def iota(shape, dim):
    return lax.broadcasted_iota(jnp.int32, shape, dim)


def onehot(cond):
    return jnp.where(cond, 1.0, 0.0).astype(BF)


def ln(x):
    mean = jnp.mean(x, axis=-1, keepdims=True)
    centred = x - mean
    inv = lax.rsqrt(jnp.mean(centred * centred, axis=-1, keepdims=True) + LN_EPS)
    return centred * inv, inv


def ln_back(scaled, inv, grad):
    mean_grad = jnp.mean(grad, axis=-1, keepdims=True)
    mean_proj = jnp.mean(grad * scaled, axis=-1, keepdims=True)
    return inv * (grad - mean_grad - scaled * mean_proj)


def gelu_pair(v):
    gauss = jnp.exp(-0.5 * v * v)
    t = 1.0 / (1.0 + (0.3275911 * 0.7071067811865476) * jnp.abs(v))
    poly = t * (
        0.127414796 + t * (-0.142248368 + t * (0.7107068705 + t * (-0.7265760135 + t * 0.5307027145)))
    )
    tail = poly * gauss
    phi = jnp.where(v < 0.0, tail, 1.0 - tail)
    return v * phi, phi + v * gauss * 0.3989422804014327


def key_target(lanes, width, shape, dim):
    y = iota(shape, dim)
    pos = y & 15
    col = jnp.where(pos < 8, pos, pos - 2)
    valid = ((pos & 7) < 6) & (y < lanes)
    return jnp.where(valid, (y >> 4) * REACH + col + (WLON - 1), -1)


def kernel(
    x_ref, ct_hbm, wqkv_hbm, wproj_hbm, wup_hbm, wdown_hbm, eb_ref,
    res_ref, gin_ref, oqkv_ref, oproj_ref, oup_ref, odown_ref, obias_ref,
    ct_ref, wqkv_ref, wproj_ref, wup_ref, wdown_ref, in_sem, win_ref, n1_ref, sc1_ref, inv1_ref, qkv_ref, p1_ref, p2_ref, mix_ref, sc2_ref, inv2_ref, n2_ref,
    act_ref, slope_ref, gpre_ref, gqkv_ref, ghb_ref, g_ref,
    t_ref, bias1_ref, bias2_ref, ds1_ref, ds2_ref,
    perm_ref, sel_ref,
    xs_ref, xr_ref,
    strip_ref, r0_ref, a_du_ref, a_qp_ref, r1_du_ref, r1_qp_ref, s2_ref, r2_ref, s3_ref, r3_ref,
    bs_ref, br_ref, ball_ref,
    x_send, x_recv, s0_send, s0_recv, s1_send, s1_recv, s2_send, s2_recv, s3_send, s3_recv,
    b_send, b_recv, bg_send, bg_recv,
):
    lat = lax.axis_index("lat")
    lon = lax.axis_index("lon")

    def at_lat(k):
        return lax.rem(lat + k + NLAT, NLAT)

    def at_lon(k):
        return lax.rem(lon + k + NLON, NLON)

    loads = [
        pltpu.make_async_copy(src, dst, in_sem.at[i])
        for i, (src, dst) in enumerate(
            (
                (wqkv_hbm, wqkv_ref),
                (wproj_hbm, wproj_ref),
                (wup_hbm, wup_ref),
                (wdown_hbm, wdown_ref),
                (ct_hbm, ct_ref),
            )
        )
    ]
    for load in loads:
        load.start()

    barrier = pltpu.get_barrier_semaphore()

    def greet_lat(k, carry):
        pl.semaphore_signal(barrier, inc=1, device_id={"lat": at_lat(k)}, device_id_type=MESH)
        return carry

    def greet_lon(k, carry):
        pl.semaphore_signal(barrier, inc=1, device_id={"lon": at_lon(k)}, device_id_type=MESH)
        return carry

    lax.fori_loop(1, NLAT, greet_lat, 0)
    lax.fori_loop(1, NLON, greet_lon, 0)
    def greet_far(k, carry):
        to = {"lat": lax.rem(lat + 2 * k, NLAT), "lon": lax.rem(lon + RING, NLON)}
        pl.semaphore_signal(barrier, inc=1, device_id=to, device_id_type=MESH)
        return carry

    lax.fori_loop(1, CHIPS, greet_far, 0)
    for k in (-1, 1):
        pl.semaphore_signal(
            barrier, inc=1, device_id={"lat": at_lat(k), "lon": at_lon(k)}, device_id_type=MESH
        )

    lane = iota((1, C), 1) >> 5
    hm = [onehot(lane == h) for h in range(HEADS)]
    eye = onehot(iota((C, C), 0) == iota((C, C), 1))
    tgt1 = key_target(TOK, 256, (1, 256), 1)
    tgt2 = key_target(96, 128, (1, 128), 1)

    def load_window(src):
        win_ref[...] = jnp.zeros((TOK, C), F32)
        for r in range(6):
            for c in range(WLON):
                v = src[r, c].astype(F32)
                for lev in range(2):
                    at = 96 * lev + 16 * r + QPOS[c]
                    win_ref[at:at + 1, :] = v[lev:lev + 1]
        return win_ref[...]

    def store_window(dst, val):
        for r in range(6):
            for c in range(WLON):
                at = 16 * r + QPOS[c]
                dst[r, c] = jnp.concatenate([val[at:at + 1], val[at + 96:at + 97]], axis=0).astype(BF)

    def group(val, lev, row, half):
        at = 96 * lev + 16 * row + 8 * half
        return val[at:at + 8]

    def strip(val, row0, half):
        return jnp.concatenate(
            [group(val, lev, row0 + r, half) for lev in range(2) for r in range(3)], axis=0
        ).astype(BF)

    def exchange_copies(idx):
        step = -1 if idx < 2 else 1
        targets = (
            {"lon": at_lon(step)},
            {"lat": at_lat(step)},
            {"lat": at_lat(step), "lon": at_lon(step)},
        )
        return [
            pltpu.make_async_remote_copy(
                src_ref=xs_ref.at[idx, i],
                dst_ref=xr_ref.at[idx, i],
                send_sem=x_send.at[idx, i],
                recv_sem=x_recv.at[idx, i],
                device_id=targets[i],
                device_id_type=MESH,
            )
            for i in range(3)
        ]

    def exchange_start(idx, val):
        if idx < 2:
            parts = (strip(val, 3, 0), strip(val, 0, 1), strip(val, 0, 0))
        else:
            parts = (strip(val, 0, 1), strip(val, 3, 0), strip(val, 3, 1))
        for i, copy in reversed(list(enumerate(exchange_copies(idx)))):
            xs_ref[idx, i] = parts[i]
            copy.start()

    def exchange_finish(idx, val):
        for copy in exchange_copies(idx):
            copy.wait()
        got = [xr_ref[idx, i].astype(F32) for i in range(3)]
        row_near = 0 if idx < 2 else 3
        half_near = 0 if idx < 2 else 1
        rows = []
        for lev in range(2):
            old = 1 - lev
            for row in range(6):
                near_row = (row < 3) == (row_near == 0)
                r = row % 3
                pieces = []
                for half in range(2):
                    near_half = half == half_near
                    at = 24 * old + 8 * r
                    if near_row and near_half:
                        piece = group(val, old, (3 if idx < 2 else 0) + r, 1 - half)
                    elif near_row:
                        piece = got[0][at:at + 8]
                    elif near_half:
                        piece = got[1][at:at + 8]
                    else:
                        piece = got[2][at:at + 8]
                    pieces.append(piece)
                rows += pieces
        return jnp.concatenate(rows, axis=0)

    def load_table(b):
        t_ref[...] = jnp.zeros_like(t_ref)
        for a in range(ZONES):
            if b == 0:
                rows = pl.ds(a, HEADS, stride=ZONES)
            else:
                rows = pl.ds(36 * (a // 6) + a % 6, HEADS, stride=6)
            for lt in range(3):
                width = min(128, TAB - 128 * lt)
                lane = TAB * a + 128 * lt
                piece = eb_ref[:, b, lane:lane + width]
                if width < 128:
                    piece = jnp.concatenate([piece, jnp.zeros((HEADS, 128 - width), F32)], axis=1)
                t_ref[lt, rows, :] = piece
        return jnp.concatenate([t_ref[lt] for lt in range(3)], axis=1)

    def split3(v):
        hi = v.astype(BF)
        rest = v - hi.astype(F32)
        mid = rest.astype(BF)
        return hi, mid, (rest - mid.astype(F32)).astype(BF)

    def expand_bias(b):
        table = load_table(b)
        if b == 0:
            spread = onehot(iota((384, 256), 0) == tgt1)
            mask = jnp.broadcast_to(jnp.where(tgt1 < 0, NEG_FILL, 0.0), (72, 256))
        else:
            spread = jnp.concatenate(
                [onehot(iota((384, 128), 0) == jnp.where(tgt2 < 0, -1, tgt2 + 138 * lv)) for lv in range(2)], axis=1
            )
            row = iota((72, 1), 0)
            row = jnp.where(row >= 36, row - 36, row)
            far_row = jnp.where(lax.rem(row, 6) >= 3, 1, 0)
            far_key = jnp.where(iota((1, 128), 1) >= 48, 1, 0)
            last = jnp.where(lat == NLAT - 1, 1, 0)
            cut = (far_row + far_key) * last == 1
            mask = jnp.where(cut | (tgt2 < 0), NEG_FILL, 0.0)
            low = iota((72, 1), 0) < 36
        for c in range(WLON):
            rolled = pltpu.roll(table, c, 1) if c else table
            full = sum(nn(p, spread) for p in split3(rolled))
            if b == 0:
                full = full + mask
                for t in range(2):
                    bias1_ref[t, pl.ds(QPOS[c], 72, stride=16), :] = full[:, 128 * t:128 * t + 128]
            else:
                bias2_ref[pl.ds(QPOS[c], 72, stride=16), :] = jnp.where(low, full[:, 0:128], full[:, 128:256]) + mask
        for p in PAD_POS:
            if b == 0:
                for t in range(2):
                    bias1_ref[t, pl.ds(p, 72, stride=16), :] = mask[:, 128 * t:128 * t + 128]
            else:
                bias2_ref[pl.ds(p, 72, stride=16), :] = mask

    def head_bias(b, h, seg):
        if b == 0:
            rows = slice(TOK * h, TOK * h + TOK)
            return jnp.concatenate([bias1_ref[0, rows, :], bias1_ref[1, rows, 0:64]], axis=1)
        at = 96 * (HEADS * seg + h)
        return bias2_ref[at:at + 96, 0:96]

    segments = ((0, TOK),), ((0, 96), (96, 96))

    def forward(b, u):
        sc1, inv1 = ln(u)
        n1 = sc1.astype(BF)
        n1_ref[b] = n1
        sc1_ref[b] = sc1
        inv1_ref[b] = inv1
        qkv_ref[b] = nn(n1, wqkv_ref[b]).astype(BF)
        q = qkv_ref[b, :, 0:C]
        k = qkv_ref[b, :, C:2 * C]
        v = qkv_ref[b, :, 2 * C:3 * C]
        cases = [(seg, slice(start, start + size), h) for seg, (start, size) in enumerate(segments[b]) for h in range(HEADS)]
        qh = [q * hm[h] for h in range(HEADS)]
        vh = [v * hm[h] for h in range(HEADS)]
        scores = [nt(qh[h][rows], k[rows]) for _, rows, h in cases]
        probs = []
        for (seg, rows, h), raw in zip(cases, scores):
            full = raw * SCALE + head_bias(b, h, seg)
            e = jnp.exp(full - jnp.max(full, axis=-1, keepdims=True))
            p = (e * (1.0 / jnp.sum(e, axis=-1, keepdims=True))).astype(BF)
            if b == 0:
                p1_ref[h] = p
            else:
                p2_ref[h, rows, :] = p
            probs.append(p)
        mixed = [None] * len(segments[b])
        for (seg, rows, h), p in zip(cases, probs):
            part = nn(p, vh[h][rows])
            mixed[seg] = part if h == 0 else mixed[seg] + part
        for seg, (start, size) in enumerate(segments[b]):
            mix_ref[b, start:start + size, :] = mixed[seg].astype(BF)
        hidden = (u + nn(mix_ref[b], wproj_ref[b])).astype(BF).astype(F32)
        sc2, inv2 = ln(hidden)
        n2 = sc2.astype(BF)
        sc2_ref[b] = sc2
        inv2_ref[b] = inv2
        n2_ref[b] = n2
        acc = hidden
        for c in range(0, HID, 256):
            act, slope = gelu_pair(nn(n2, wup_ref[b, :, c:c + 256]))
            act = act.astype(BF)
            act_ref[b, :, c:c + 256] = act
            slope_ref[b, :, c:c + 256] = slope.astype(BF)
            acc = acc + nt(act, wdown_ref[b, :, c:c + 256])
        return acc.astype(BF).astype(F32)

    def backward_mlp(b, gf):
        g = gf.astype(BF)
        g_ref[b] = g
        gn2 = jnp.zeros((TOK, C), F32)
        for c in range(0, HID, 256):
            gact = nn(g, wdown_ref[b, :, c:c + 256])
            gpre = (gact * slope_ref[b, :, c:c + 256].astype(F32)).astype(BF)
            gpre_ref[b, :, c:c + 256] = gpre
            gn2 = gn2 + nt(gpre, wup_ref[b, :, c:c + 256])
        ghid = gf + ln_back(sc2_ref[b], inv2_ref[b], gn2)
        ghb_ref[b] = ghid.astype(BF)
        return ghid

    def attention_start(b):
        gmix = nt(ghb_ref[b], wproj_ref[b]).astype(BF)
        q = qkv_ref[b, :, 0:C]
        v = qkv_ref[b, :, 2 * C:3 * C]
        cases = [(seg, slice(start, start + size), h) for seg, (start, size) in enumerate(segments[b]) for h in range(HEADS)]
        gh = [gmix * hm[h] for h in range(HEADS)]
        gps = [nt(gh[h][rows], v[rows]) for _, rows, h in cases]
        spans = [slice(start, start + size) for start, size in segments[b]]
        qt = [nt(eye, q[rows]).astype(BF) for rows in spans]
        gmt = [nt(eye, gmix[rows]).astype(BF) for rows in spans]
        return cases, gps, qt, gmt

    def attention_grads(b, started):
        cases, gps, qt, gmt = started
        k = qkv_ref[b, :, C:2 * C]
        kh = [k * hm[h] for h in range(HEADS)]
        gvt = []
        dsbs = []
        for (seg, rows, h), gp in zip(cases, gps):
            pb = p1_ref[h] if b == 0 else p2_ref[h, rows, :]
            gvt.append(nn(gmt[seg][32 * h:32 * h + 32], pb))
            pf = pb.astype(F32)
            ds = pf * (gp - jnp.sum(gp * pf, axis=-1, keepdims=True))
            if b == 0:
                ds1_ref[0, TOK * h:TOK * h + TOK, :] = ds[:, 0:128]
                ds1_ref[1, TOK * h:TOK * h + TOK, 0:64] = ds[:, 128:192]
            else:
                at = 96 * (HEADS * seg + h)
                ds2_ref[at:at + 96, 0:96] = ds
            dsbs.append(ds.astype(BF))
        gkt = [nn(qt[seg][32 * h:32 * h + 32], dsb) for (seg, _, h), dsb in zip(cases, dsbs)]
        gq = [None] * len(segments[b])
        for (seg, rows, h), dsb in zip(cases, dsbs):
            part = nn(dsb, kh[h][rows])
            gq[seg] = part if h == 0 else gq[seg] + part
        for seg, (start, size) in enumerate(segments[b]):
            rows = slice(start, start + size)
            heads = slice(HEADS * seg, HEADS * seg + HEADS)
            small = eye if size == C else eye[0:size, 0:size]
            gk = nt(small, (jnp.concatenate(gkt[heads], axis=0) * SCALE).astype(BF)).astype(BF)
            gv = nt(small, jnp.concatenate(gvt[heads], axis=0).astype(BF)).astype(BF)
            gqkv_ref[b, rows, 0:C] = (gq[seg] * SCALE).astype(BF)
            gqkv_ref[b, rows, C:2 * C] = gk
            gqkv_ref[b, rows, 2 * C:3 * C] = gv

    def input_grad(b, ghid):
        gn1 = nt(gqkv_ref[b], wqkv_ref[b])
        return (ghid + ln_back(sc1_ref[b], inv1_ref[b], gn1)).astype(BF).astype(F32)

    def put_strips(b, t, s, val):
        val = (val * NORM).astype(BF)
        for i in range(val.shape[1] // 128):
            strip_ref[b, t, s + i] = val[:, 128 * i:128 * i + 128]

    def grads_mlp(b):
        actt = nt(perm_ref[...], act_ref[b]).astype(BF)
        g = g_ref[b]
        for pair in range(2):
            at = 384 * pair
            both = [nn(actt[at + 192 * i:at + 192 * i + 192], g) for i in range(2)]
            put_strips(b, 0, 3 * pair, jnp.concatenate(both, axis=1))
        n2t = nt(eye, n2_ref[b]).astype(BF)
        for s in range(3):
            put_strips(b, 1, 2 * s, nn(n2t, gpre_ref[b, :, 256 * s:256 * s + 256]))

    def grads_attention(b):
        n1t = nt(eye, n1_ref[b]).astype(BF)
        mixt = nt(eye, mix_ref[b]).astype(BF)
        put_strips(b, 2, 0, nn(n1t, gqkv_ref[b, :, 0:256]))
        put_strips(b, 2, 2, nn(n1t, gqkv_ref[b, :, 256:512]))
        rest = [nn(n1t, gqkv_ref[b, :, 512:576]), nn(mixt, ghb_ref[b])]
        put_strips(b, 2, 4, jnp.concatenate(rest, axis=1))

    core = lax.rem(lat, 2)
    chip = lat // 2
    ring = lon // RING
    z = lax.rem(lon, RING)
    half = C // 2
    a_refs = (a_du_ref, a_qp_ref)

    def far_first(i):
        step = (i + 1) // 2
        return lax.rem(z + RING // 2 + step * (1 - 2 * lax.rem(i, 2)), RING)

    r1_refs = (r1_du_ref, r1_qp_ref)

    def far_first_lat(i):
        step = (i + 1) // 2
        return lax.rem(lat + NLAT // 2 + step * (1 - 2 * lax.rem(i, 2)), NLAT)

    def place(b):
        return chip if b else lax.rem(chip + 4, 8)

    def owned(b, kind):
        at = place(b)
        if kind == 0:
            return at // 3 == core, at - 3 * core
        return (at >= 6) | (at == 3 - 3 * core), jnp.where(at >= 6, at - 6, 2)

    def owner(b, kind, i):
        if kind == 0:
            at = 3 * core + i
        else:
            at = 6 + i if i < 2 else 3 - 3 * core
        at = at if b else lax.rem(at + 4, 8)
        return 2 * at + core

    def wait_bytes(ref, sem):
        pltpu.make_async_copy(ref, ref, sem).wait()

    def s0_copy(b, t):
        return pltpu.make_async_remote_copy(
            src_ref=strip_ref.at[b, t, pl.ds(3 - 3 * core, 3)],
            dst_ref=r0_ref.at[b, t],
            send_sem=s0_send.at[b, t],
            recv_sem=s0_recv.at[b, t],
            device_id={"lat": lat + 1 - 2 * core},
            device_id_type=MESH,
        )

    def stage0_send(b, t):
        s0_copy(b, t).start()

    def s1_copy(b, kind, i, g):
        return pltpu.make_async_remote_copy(
            src_ref=a_refs[kind].at[b, i, g],
            dst_ref=r1_refs[kind].at[b, CHIPS * ring + chip],
            send_sem=s1_send.at[b, kind, i, g],
            recv_sem=s1_recv.at[b, kind],
            device_id={"lat": owner(b, kind, i), "lon": RING * g + z},
            device_id_type=MESH,
        )

    def s1_here(b, kind, i, g):
        return (lat == owner(b, kind, i)) & (ring == g)

    def stage1_send(b, kind):
        groups = (0, 1) if kind == 0 else (2,)
        for t in groups:
            s0_copy(b, t).wait_recv()
        for i in range(3):
            for part, t in enumerate(groups):
                both = strip_ref[b, t, 3 * core + i].astype(F32) + r0_ref[b, t, i].astype(F32)
                for g in range(2):
                    a_refs[kind][b, i, g, part] = both[half * g:half * g + half].astype(BF)
            for g in range(2):
                here = s1_here(b, kind, i, g)

                @pl.when(jnp.logical_not(here))
                def _():
                    s1_copy(b, kind, i, g).start()

                @pl.when(here)
                def _():
                    r1_refs[kind][b, CHIPS * ring + chip] = a_refs[kind][b, i, g]

    def stage1_reduce(b, kind):
        mine, _ = owned(b, kind)
        parts = 2 if kind == 0 else 1

        @pl.when(mine)
        def _():
            ref = r1_refs[kind]
            wait_bytes(ref.at[b, pl.ds(0, 2 * CHIPS - 1)], s1_recv.at[b, kind])
            spread = []
            for part in range(parts):
                acc = ref[b, 0, part].astype(F32)
                for i in range(1, 2 * CHIPS):
                    acc = acc + ref[b, i, part].astype(F32)
                spread.append(nn(sel_ref[...], acc.astype(BF)))
            if parts == 1:
                spread.append(jnp.zeros((8 * RING, 128), F32))
            for j in range(RING):
                tile = jnp.concatenate([v[8 * j:8 * j + 8] for v in spread], axis=0)
                s2_ref[b, kind, j] = tile.astype(BF)
            r2_ref[b, kind, z] = s2_ref[b, kind, z]

            def send(i, carry):
                to = far_first(i)
                pltpu.make_async_remote_copy(
                    src_ref=s2_ref.at[b, kind, to],
                    dst_ref=r2_ref.at[b, kind, z],
                    send_sem=s2_send.at[b, kind],
                    recv_sem=s2_recv.at[b, kind],
                    device_id={"lon": RING * ring + to},
                    device_id_type=MESH,
                ).start()
                return carry

            lax.fori_loop(0, RING - 1, send, 0)

    def stage2_reduce(b, kind):
        mine, i = owned(b, kind)
        which = 3 * core + i

        @pl.when(mine)
        def _():
            wait_bytes(r2_ref.at[b, kind, pl.ds(0, RING - 1)], s2_recv.at[b, kind])
            acc = r2_ref[b, kind, 0].astype(F32)
            for j in range(1, RING):
                acc = acc + r2_ref[b, kind, j].astype(F32)
            total = acc.astype(BF)
            s3_ref[b, kind] = total
            r3_ref[b, kind, which] = total

            def send(i, carry):
                pltpu.make_async_remote_copy(
                    src_ref=s3_ref.at[b, kind],
                    dst_ref=r3_ref.at[b, kind, which],
                    send_sem=s3_send.at[b, kind],
                    recv_sem=s3_recv.at[b, kind],
                    device_id={"lat": far_first_lat(i)},
                    device_id_type=MESH,
                ).start()
                return carry

            lax.fori_loop(0, NLAT - 1, send, 0)

    def put_rows(ref, b, val):
        for i in range(SHARD):
            ref[i, b:b + 1, :] = val[i:i + 1]

    def stage3_finish(b, kind):
        mine, _ = owned(b, kind)

        @pl.when(mine)
        def _():
            wait_bytes(r3_ref.at[b, kind, pl.ds(0, 5)], s3_recv.at[b, kind])

        @pl.when(jnp.logical_not(mine))
        def _():
            wait_bytes(r3_ref.at[b, kind], s3_recv.at[b, kind])

        tiles = [r3_ref[b, kind, s].astype(F32) for s in range(6)]
        first = jnp.concatenate([v[0:8] for v in tiles], axis=1)
        if kind == 0:
            for s in range(4):
                part = first[:, 192 * s:192 * s + 192]
                for i in range(SHARD):
                    odown_ref[b, 4 * i + s:4 * i + s + 1, :] = part[i:i + 1]
            put_rows(oup_ref, b, jnp.concatenate([v[8:16] for v in tiles], axis=1))
        else:
            put_rows(oqkv_ref, b, first[:, 0:576])
            put_rows(oproj_ref, b, first[:, 576:768])

    def stages_sent(b):
        for t in range(3):
            s0_copy(b, t).wait_send()
        for kind in range(2):
            for i in range(3):
                for g in range(2):
                    @pl.when(jnp.logical_not(s1_here(b, kind, i, g)))
                    def _():
                        s1_copy(b, kind, i, g).wait_send()

            @pl.when(owned(b, kind)[0])
            def _():
                wait_bytes(s2_ref.at[b, kind, pl.ds(0, RING - 1)], s2_send.at[b, kind])
                wait_bytes(s2_ref.at[b, kind, pl.ds(0, NLAT - 1)], s3_send.at[b, kind])

    tiles = (11, 6)
    tile0 = (0, 11)

    def bias_home(b, i):
        return RING * (i % 2) + 3 * (i // 2) + b

    def bias_mine(b):
        i = 2 * (z // 3) + ring
        return (lax.rem(z, 3) == b) & (i < tiles[b]), i

    def fold_bias(b):
        total = None
        width = 384 if b == 0 else 256
        if b == 0:
            spread = onehot(iota((C, 384), 1) == key_target(TOK, 256, (C, 1), 0))
        else:
            spread = onehot(iota((96, 256), 1) == key_target(96, 128, (96, 1), 0))
        for c in range(WLON):
            if b == 0:
                got = [ds1_ref[t, pl.ds(QPOS[c], 72, stride=16), :].astype(BF) for t in range(2)]
                part = nn(got[0], spread[0:128]) + nn(got[1][:, 0:64], spread[128:C])
            else:
                part = nn(ds2_ref[pl.ds(QPOS[c], 72, stride=16), :].astype(BF)[:, 0:96], spread)
            if c:
                part = pltpu.roll(part, width - c, 1)
            total = part if total is None else total + part
        total = jnp.concatenate([total, jnp.zeros((8, width), F32)], axis=0)
        lanes = width // 128 - 1
        extra = TAB - 256 if b == 0 else 138 - 128
        for rt in range(5):
            for lt in range(lanes):
                tile = total[16 * rt:16 * rt + 16, 128 * lt:128 * lt + 128]
                bs_ref[tile0[b] + rt * lanes + lt] = tile.astype(BF)
        packed = None
        for rt in range(5):
            tile = total[16 * rt:16 * rt + 16, 128 * lanes:]
            if rt:
                tile = pltpu.roll(tile, extra * rt, 1)
                packed = jnp.where(iota((16, 128), 1) >= extra * rt, tile, packed)
            else:
                packed = tile
        bs_ref[tile0[b] + 5 * lanes] = packed.astype(BF)

    def b_copy(b, i):
        return pltpu.make_async_remote_copy(
            src_ref=bs_ref.at[tile0[b] + i],
            dst_ref=br_ref.at[lon],
            send_sem=b_send.at[tile0[b] + i],
            recv_sem=b_recv,
            device_id={"lon": bias_home(b, i)},
            device_id_type=MESH,
        )

    def bias_send(b):
        for i in range(tiles[b]):
            @pl.when(lon != bias_home(b, i))
            def _():
                b_copy(b, i).start()

            @pl.when(lon == bias_home(b, i))
            def _():
                br_ref[lon] = bs_ref[tile0[b] + i]

    def bias_reduce(b):
        mine, i = bias_mine(b)
        at = tile0[b] + i

        @pl.when(mine)
        def _():
            wait_bytes(br_ref.at[pl.ds(0, NLON - 1)], b_recv)
            acc = br_ref[0].astype(F32)
            for j in range(1, NLON):
                acc = acc + br_ref[j].astype(F32)
            ball_ref[at] = acc.astype(BF)

            def send_to(to):
                pltpu.make_async_remote_copy(
                    src_ref=ball_ref.at[at],
                    dst_ref=ball_ref.at[at],
                    send_sem=bg_send,
                    recv_sem=bg_recv.at[b],
                    device_id={"lon": to},
                    device_id_type=MESH,
                ).start()

            def send(i, carry):
                to = far_first(i)
                send_to(RING * (1 - ring) + to)
                send_to(RING * ring + to)
                return carry

            lax.fori_loop(0, RING - 1, send, 0)
            send_to(RING * (1 - ring) + z)

    def bias_finish(b):
        mine, _ = bias_mine(b)

        @pl.when(mine)
        def _():
            wait_bytes(ball_ref.at[pl.ds(tile0[b], tiles[b] - 1)], bg_recv.at[b])

        @pl.when(jnp.logical_not(mine))
        def _():
            wait_bytes(ball_ref.at[pl.ds(tile0[b], tiles[b])], bg_recv.at[b])

        lanes = 2 if b == 0 else 1
        extra = TAB - 256 if b == 0 else 138 - 128
        packed = ball_ref[tile0[b] + 5 * lanes].astype(F32)
        for rt in range(5):
            rows = [ball_ref[tile0[b] + rt * lanes + lt].astype(F32) for lt in range(lanes)]
            rows.append(pltpu.roll(packed, 128 - extra * rt, 1) if rt else packed)
            for i in range(16 if rt < 4 else 8):
                at = 16 * rt + i
                if b == 0:
                    h, a = at // ZONES, at % ZONES
                    for lt in range(3):
                        width = min(128, TAB - 128 * lt)
                        lane = TAB * a + 128 * lt
                        obias_ref[0, h, :, lane:lane + width] = rows[lt][i:i + 1, 0:width]
                else:
                    level, h, a = at // 36, at % 36 // 6, at // 36 * 6 + at % 6
                    for lt in range(2):
                        width = min(128, 138 - 128 * lt)
                        lane = TAB * a + 138 * level + 128 * lt
                        obias_ref[1, h, :, lane:lane + width] = rows[lt][i:i + 1, 0:width]

    def bias_sent(b):
        for i in range(tiles[b]):
            @pl.when(lon != bias_home(b, i))
            def _():
                b_copy(b, i).wait_send()

        @pl.when(bias_mine(b)[0])
        def _():
            wait_bytes(br_ref.at[pl.ds(0, NLON - 1)], bg_send)

    expand_bias(0)
    u1 = load_window(x_ref)
    for load in loads[:4]:
        load.wait()
    out1 = forward(0, u1)
    pl.semaphore_wait(barrier, NLAT - 1 + NLON - 1 + CHIPS - 1 + 2)
    exchange_start(1, out1)
    loads[4].wait()
    ct = load_window(ct_ref)
    exchange_start(0, ct)
    expand_bias(1)
    for s in range(4):
        perm_ref[192 * s:192 * s + 192, :] = onehot(iota((192, HID), 1) == 4 * iota((192, HID), 0) + s)
    row = iota((8 * RING, 1), 0)
    pos = row & 7
    sel_ref[...] = onehot(iota((8 * RING, C // 2), 1) == jnp.where(pos < SHARD, (row >> 3) * SHARD + pos, -1))
    obias_ref[1] = jnp.zeros((HEADS, 1, ZONES * TAB), F32)
    u2 = exchange_finish(1, out1)
    out2 = forward(1, u2)
    exchange_start(2, out2)
    g2 = exchange_finish(0, ct)
    ghid2 = backward_mlp(1, g2)
    attention_grads(1, attention_start(1))
    gsec = input_grad(1, ghid2)
    exchange_start(3, gsec)
    grads_mlp(1)
    stage0_send(1, 0)
    stage0_send(1, 1)
    grads_attention(1)
    stage0_send(1, 2)
    fold_bias(1)
    bias_send(1)
    stage1_send(1, 0)
    stage1_send(1, 1)
    store_window(res_ref, exchange_finish(2, out2))
    g1 = exchange_finish(3, gsec)
    ghid1 = backward_mlp(0, g1)
    grads_mlp(0)
    stage0_send(0, 0)
    stage0_send(0, 1)
    started = attention_start(0)
    stage1_send(0, 0)
    attention_grads(0, started)
    grads_attention(0)
    stage0_send(0, 2)
    fold_bias(0)
    bias_send(0)
    stage1_send(0, 1)
    stage1_reduce(1, 0)
    stage1_reduce(1, 1)
    bias_reduce(1)
    store_window(gin_ref, input_grad(0, ghid1))
    stage1_reduce(0, 0)
    stage1_reduce(0, 1)
    bias_reduce(0)
    stage2_reduce(1, 0)
    stage2_reduce(1, 1)
    bias_finish(1)
    stage2_reduce(0, 0)
    stage2_reduce(0, 1)
    stage3_finish(1, 0)
    stage3_finish(1, 1)
    bias_finish(0)
    stage3_finish(0, 0)
    stage3_finish(0, 1)
    for b in range(2):
        stages_sent(b)
        bias_sent(b)


def on_device(inputs, cotangent, w_qkv, w_proj, w_up, w_down, earth_bias):
    vm = pl.BlockSpec(memory_space=pltpu.VMEM)
    hbm = pl.BlockSpec(memory_space=pltpu.HBM)
    shapes = (
        jax.ShapeDtypeStruct((6, WLON, 2, C), BF),
        jax.ShapeDtypeStruct((6, WLON, 2, C), BF),
        jax.ShapeDtypeStruct((SHARD, 2, 576), F32),
        jax.ShapeDtypeStruct((SHARD, 2, 192), F32),
        jax.ShapeDtypeStruct((SHARD, 2, 768), F32),
        jax.ShapeDtypeStruct((2, 24, 192), F32),
        jax.ShapeDtypeStruct((2, HEADS, 1, 3312), F32),
    )
    outs = pl.pallas_call(
        kernel,
        out_shape=shapes,
        in_specs=[vm, hbm, hbm, hbm, hbm, hbm, vm],
        out_specs=(vm,) * 7,
        scratch_shapes=[
            pltpu.VMEM((6, WLON, 2, C), BF),
            pltpu.VMEM((2, C, 576), BF),
            pltpu.VMEM((2, C, C), BF),
            pltpu.VMEM((2, C, HID), BF),
            pltpu.VMEM((2, C, HID), BF),
            pltpu.SemaphoreType.DMA((5,)),
            pltpu.VMEM((TOK, C), F32),
            pltpu.VMEM((2, TOK, C), BF),
            pltpu.VMEM((2, TOK, C), F32),
            pltpu.VMEM((2, TOK, 1), F32),
            pltpu.VMEM((2, TOK, 576), BF),
            pltpu.VMEM((HEADS, TOK, TOK), BF),
            pltpu.VMEM((HEADS, TOK, 96), BF),
            pltpu.VMEM((2, TOK, C), BF),
            pltpu.VMEM((2, TOK, C), F32),
            pltpu.VMEM((2, TOK, 1), F32),
            pltpu.VMEM((2, TOK, C), BF),
            pltpu.VMEM((2, TOK, HID), BF),
            pltpu.VMEM((2, TOK, HID), BF),
            pltpu.VMEM((2, TOK, HID), BF),
            pltpu.VMEM((2, TOK, 576), BF),
            pltpu.VMEM((2, TOK, C), BF),
            pltpu.VMEM((2, TOK, C), BF),
            pltpu.VMEM((3, 72, 128), F32),
            pltpu.VMEM((2, 1152, 128), F32),
            pltpu.VMEM((1152, 128), F32),
            pltpu.VMEM((2, 1152, 128), F32),
            pltpu.VMEM((1152, 128), F32),
            pltpu.VMEM((HID, HID), BF),
            pltpu.VMEM((8 * RING, C // 2), BF),
            pltpu.VMEM((4, 3, 48, C), BF),
            pltpu.VMEM((4, 3, 48, C), BF),
            pltpu.VMEM((2, 3, 6, C, 128), BF),
            pltpu.VMEM((2, 3, 3, C, 128), BF),
            pltpu.VMEM((2, 3, 2, 2, C // 2, 128), BF),
            pltpu.VMEM((2, 3, 2, 1, C // 2, 128), BF),
            pltpu.VMEM((2, 2 * CHIPS, 2, C // 2, 128), BF),
            pltpu.VMEM((2, 2 * CHIPS, 1, C // 2, 128), BF),
            pltpu.VMEM((2, 2, RING, 16, 128), BF),
            pltpu.VMEM((2, 2, RING, 16, 128), BF),
            pltpu.VMEM((2, 2, 16, 128), BF),
            pltpu.VMEM((2, 2, 6, 16, 128), BF),
            pltpu.VMEM((17, 16, 128), BF),
            pltpu.VMEM((NLON, 16, 128), BF),
            pltpu.VMEM((17, 16, 128), BF),
            pltpu.SemaphoreType.DMA((4, 3)),
            pltpu.SemaphoreType.DMA((4, 3)),
            pltpu.SemaphoreType.DMA((2, 3)),
            pltpu.SemaphoreType.DMA((2, 3)),
            pltpu.SemaphoreType.DMA((2, 2, 3, 2)),
            pltpu.SemaphoreType.DMA((2, 2)),
            pltpu.SemaphoreType.DMA((2, 2)),
            pltpu.SemaphoreType.DMA((2, 2)),
            pltpu.SemaphoreType.DMA((2, 2)),
            pltpu.SemaphoreType.DMA((2, 2)),
            pltpu.SemaphoreType.DMA((17,)),
            pltpu.SemaphoreType.DMA,
            pltpu.SemaphoreType.DMA,
            pltpu.SemaphoreType.DMA((2,)),
        ],
        compiler_params=pltpu.CompilerParams(
            collective_id=0, has_side_effects=True, vmem_limit_bytes=64 * 1024 * 1024
        ),
        name="earth_blocks",
    )(
        inputs.transpose(1, 2, 0, 3),
        cotangent.transpose(1, 2, 0, 3),
        w_qkv,
        w_proj,
        w_up,
        w_down.transpose(0, 2, 1),
        earth_bias.reshape(2, HEADS, 3312).transpose(1, 0, 2),
    )
    result, grad_inputs, g_qkv, g_proj, g_up, g_down, g_bias = outs
    return (
        result.transpose(2, 0, 1, 3),
        grad_inputs.transpose(2, 0, 1, 3),
        g_qkv.transpose(1, 0, 2),
        g_proj.transpose(1, 0, 2),
        g_up.transpose(1, 0, 2),
        g_down,
        g_bias.reshape(2, 1, 1, HEADS, 3312),
    )


def solution(mesh):
    field = P(None, "lat", "lon", None)
    shard = P(None, "lon", None)
    bias = P(None, "lat", None, None, None)
    return jax.shard_map(
        on_device,
        mesh=mesh,
        in_specs=(field, field, P(), P(), P(), P(), bias),
        out_specs=(field, field, shard, shard, shard, shard, bias),
        check_vma=False,
    )
```
